32 devices in a mesh: groups: 2 (over y), slab: 8 (over z, x), node: 2 (over core).
Axes of the slice: x: 2, y: 2, z: 4, core: 2. Of those that a mesh axis runs over, the one named last changes fastest.
Arguments:
- field_seeds: int32 [4], P(('groups', 'node')), parts along dimension 0, may hold values from 0 to 65520
- quad_weight: int32 [4], P('groups'), parts along dimension 0, may hold values from 1 to 9
- recharge: float32 [64, 64, 256], P(('groups', 'slab')), parts along dimension 0, may hold values from -16 to 16
- well_cells: int32 [128], P(('groups', 'slab')), parts along dimension 0, may hold values from 0 to 65535
- well_rates: float32 [128], P(('groups', 'slab')), parts along dimension 0, may hold values from -20 to 20
- sensitivity: float32 [64, 64, 256], P(('groups', 'slab')), parts along dimension 0, may hold values from -24 to 24
Outputs:
- head_field: float32 [4, 32, 64, 256], P(('groups', 'node'), 'slab'), parts along dimension 0
- adjoint_field: float32 [4, 32, 64, 256], P(('groups', 'node'), 'slab'), parts along dimension 0
- zone_gradient: float32 [16, 16, 64], P(('groups', 'slab')), parts along dimension 0
The draws below stay inside these ranges and needn't reach their ends.
There are 2 independent parts, one for each index of `groups`. The reference program is written for one: setup_inputs(seed, part) draws one part's arguments, and reference() takes and returns one part's arrays. A program takes and returns all parts, laid end to end along the dimension named above; each array names one. Nothing has to cross between parts.
All inputs are finite; a program needn't handle non-finite values.
Results may differ from the reference program's by a relative error of at most 0.0003.
Values sent between devices are 32-bit elements; how exact they have to be, the bound alone decides.
A program may use at most 192 MiB of HBM per device.

```python
import jax
import jax.numpy as jnp
from jax import lax

CX = 4
NY = 64
NZ = 256
LEVELS = 5
SWEEPS = 2
COARSE_SWEEPS = 8
WELLS_DEV = 8
NX = 32
NODES = 2
WELLS = 64
N_SLAB = 8


def draw_recharge(key, part):
    values = 4.0 * jax.random.truncated_normal(key, -4.0, 4.0, (NX, NY, NZ), jnp.float32)
    return values


def place_ends(values, key, low, high):
    place = [jax.random.randint(jax.random.fold_in(key, axis), (), 0, length) for axis, length in enumerate(values.shape)]
    main_axis = values.shape.index(max(values.shape))
    next_to = place[:main_axis] + [(place[main_axis] + 1) % values.shape[main_axis]] + place[main_axis + 1:]
    return values.at[tuple(place)].set(low).at[tuple(next_to)].set(high)


def block_scale(stream_key, shape, cuts, smallest, high):
    def one(dim, blocks):
        draws = jax.random.uniform(jax.random.fold_in(jax.random.fold_in(stream_key, 6), dim), (blocks,), jnp.float32, smallest / len(cuts), high / len(cuts))
        return jnp.repeat(jnp.exp(draws), shape[dim] // blocks).reshape((-1,) + (1,) * (len(shape) - dim - 1))

    loudness = one(*cuts[0])
    for cut in cuts[1:]:
        loudness = loudness * one(*cut)
    return loudness


def scatter_about(stream_key, shape, scale, most, pieces=(), kind=jnp.bfloat16):
    drawn = scale * jax.random.normal(stream_key, shape, jnp.float32)
    if pieces:
        drawn = drawn * block_scale(stream_key, shape, pieces, -0.22, 0.18)
    return jnp.clip(drawn, -most, most).astype(kind)


def setup_inputs(seed: int = 0, part: int = 0) -> dict:
    splits = jax.random.split(jax.random.key(seed), 7)
    part_keys = jax.random.split(jax.random.fold_in(splits[6], part), 7)
    field_seeds = jax.random.randint(part_keys[0], (NODES,), 0, 65521).astype(jnp.int32)
    quad_weight = jax.random.randint(part_keys[1], (NODES,), 1, 10).astype(jnp.int32)
    recharge = draw_recharge(jax.random.fold_in(jax.random.fold_in(splits[6], part), 71), part)
    well_cells = place_ends(jax.random.randint(part_keys[3], (WELLS,), 0, CX * NY * NZ), jax.random.fold_in(part_keys[3], 1), 0, (CX * NY * NZ) - 1).astype(jnp.int32)
    well_rates = jnp.clip(jax.random.uniform(part_keys[4], (WELLS,), jnp.float32, -20.0, 20.0) * block_scale(part_keys[4], (WELLS,), ((0, 8),), -0.4, 0.0), -20.0, 20.0)
    sensitivity = scatter_about(part_keys[5], (NX, NY, NZ), 4.0, 24.0, ((0, 8),), jnp.float32)
    return {"field_seeds": field_seeds, "quad_weight": quad_weight, "recharge": recharge, "well_cells": well_cells, "well_rates": well_rates, "sensitivity": sensitivity}


OMEGA = 0.8


def log_conductivity(seed_value, width_x, width_y, width_z, x_start):
    extent = (width_x, width_y, width_z)
    index_x = lax.broadcasted_iota(jnp.int32, extent, 0) + x_start
    index_y = lax.broadcasted_iota(jnp.int32, extent, 1)
    index_z = lax.broadcasted_iota(jnp.int32, extent, 2)
    position = (index_x * NY + index_y) * NZ + index_z
    hashed = position * 747796405 + seed_value * 277803737 + 1013904223
    hashed = jnp.bitwise_xor(hashed, lax.shift_right_logical(hashed, jnp.full(extent, 15, jnp.int32)))
    hashed = hashed * 1274126177
    hashed = jnp.bitwise_xor(hashed, lax.shift_right_logical(hashed, jnp.full(extent, 13, jnp.int32)))
    low_bits = jnp.bitwise_and(hashed, 65535)
    return 3.0 * (low_bits.astype(jnp.float32) / 65536.0) - 1.5


def restrict_all(values):
    leading = values.shape[:-3]
    width_x, width_y, width_z = values.shape[-3:]
    offset = len(leading)
    blocks = values.reshape(leading + (width_x // 2, 2, width_y // 2, 2, width_z // 2, 2))
    return jnp.sum(blocks, axis=(offset + 1, offset + 3, offset + 5)) * 0.125


def prolong_all(values):
    for axis_no in (-3, -2, -1):
        values = jnp.repeat(values, 2, axis=axis_no)
    return values


def build_operator(padded_logk, low_edge, high_edge, level_scale):
    center = padded_logk[1:-1]
    exp_center = jnp.exp(center)
    face_x = jnp.exp(0.5 * (padded_logk[:-1] + padded_logk[1:]))
    face_x = jnp.concatenate([jnp.where(low_edge, 2.0 * exp_center[:1], face_x[:1]), face_x[1:-1],
                              jnp.where(high_edge, 2.0 * exp_center[-1:], face_x[-1:])], 0)
    inner_y = jnp.exp(0.5 * (center[:, :-1] + center[:, 1:]))
    face_y = jnp.concatenate([2.0 * exp_center[:, :1], inner_y, 2.0 * exp_center[:, -1:]], 1)
    inner_z = jnp.exp(0.5 * (center[..., :-1] + center[..., 1:]))
    zeros_z = jnp.zeros_like(center[..., :1])
    face_up = jnp.concatenate([inner_z, zeros_z], 2)
    face_down = jnp.concatenate([zeros_z, inner_z], 2)
    diagonal = face_x[:-1] + face_x[1:] + face_y[:, :-1] + face_y[:, 1:] + face_down + face_up
    inverse = OMEGA / (level_scale * diagonal)
    return (face_x, face_y, face_up, face_down, diagonal, inverse, level_scale)


def apply_operator(operator_set, padded):
    face_x, face_y, face_up, face_down, diagonal, inverse, level_scale = operator_set
    values = padded[:, 1:-1]
    offdiag = face_x[:-1] * padded[:, :-2] + face_x[1:] * padded[:, 2:]
    zeros_y = jnp.zeros_like(values[:, :, :1])
    offdiag = offdiag + face_y[:, :-1] * jnp.concatenate([zeros_y, values[:, :, :-1]], 2)
    offdiag = offdiag + face_y[:, 1:] * jnp.concatenate([values[:, :, 1:], zeros_y], 2)
    zeros_z = jnp.zeros_like(values[..., :1])
    offdiag = offdiag + face_down * jnp.concatenate([zeros_z, values[..., :-1]], 3)
    offdiag = offdiag + face_up * jnp.concatenate([values[..., 1:], zeros_z], 3)
    return level_scale * (diagonal * values - offdiag)


def vcycle(level_at, source, operators, pad_fn, coarse_fn):
    operator_set = operators[level_at]
    inverse = operator_set[5]
    iterate = inverse * source
    if level_at == LEVELS - 1:
        for sweep_no in range(COARSE_SWEEPS - 1):
            iterate = iterate + inverse * (source - apply_operator(operator_set, pad_fn(iterate)))
        return iterate
    for sweep_no in range(SWEEPS - 1):
        iterate = iterate + inverse * (source - apply_operator(operator_set, pad_fn(iterate)))
    residue = source - apply_operator(operator_set, pad_fn(iterate))
    iterate = iterate + coarse_fn(level_at, residue)
    for sweep_no in range(SWEEPS):
        iterate = iterate + inverse * (source - apply_operator(operator_set, pad_fn(iterate)))
    return iterate


def zero_pad(values):
    return jnp.pad(values, ((0, 0), (1, 1), (0, 0), (0, 0)))


def cell_gradient(operator_set, head_pad, adj_pad, low_edge, high_edge):
    face_x, face_y, face_up = operator_set[0], operator_set[1], operator_set[2]
    heads_in = head_pad[1:-1]
    adj_in = adj_pad[1:-1]
    width_x, width_y = heads_in.shape[0], heads_in.shape[1]
    ones_cell = jnp.ones((1, 1, 1), head_pad.dtype)
    prod_x = face_x * (head_pad[:-1] - head_pad[1:]) * (adj_pad[:-1] - adj_pad[1:])
    weight_x = jnp.concatenate([jnp.where(low_edge, 1.0, 0.5) * ones_cell,
                                jnp.full((width_x - 1, 1, 1), 0.5, dtype=head_pad.dtype),
                                jnp.where(high_edge, 1.0, 0.5) * ones_cell], 0)
    prod_x = prod_x * weight_x
    grad_x = prod_x[:-1] + prod_x[1:]
    zeros_y = jnp.zeros_like(heads_in[:, :1])
    head_y = jnp.concatenate([zeros_y, heads_in, zeros_y], 1)
    adj_y = jnp.concatenate([zeros_y, adj_in, zeros_y], 1)
    prod_y = face_y * (head_y[:, :-1] - head_y[:, 1:]) * (adj_y[:, :-1] - adj_y[:, 1:])
    weight_y = jnp.concatenate([ones_cell, jnp.full((1, width_y - 1, 1), 0.5, dtype=head_pad.dtype), ones_cell], 1)
    prod_y = prod_y * weight_y
    grad_y = prod_y[:, :-1] + prod_y[:, 1:]
    zeros_z = jnp.zeros_like(heads_in[..., :1])
    up_head = jnp.concatenate([heads_in[..., 1:], zeros_z], 2)
    up_adj = jnp.concatenate([adj_in[..., 1:], zeros_z], 2)
    prod_z = face_up * (heads_in - up_head) * (adj_in - up_adj)
    grad_z = 0.5 * (prod_z + jnp.concatenate([zeros_z, prod_z[..., :-1]], 2))
    return -(grad_x + grad_y + grad_z)


def zone_total(cells):
    width_x, width_y, width_z = cells.shape
    blocks = cells.reshape(width_x // 4, 4, width_y // 4, 4, width_z // 4, 4)
    return jnp.sum(blocks, axis=(1, 3, 5))


def reference(field_seeds, quad_weight, recharge, well_cells, well_rates, sensitivity):
    flat_rows = recharge.reshape(N_SLAB, CX * NY * NZ)
    owner = (jnp.arange(WELLS, dtype=jnp.int32) // WELLS_DEV).astype(jnp.int32)
    source = flat_rows.at[owner, well_cells].add(well_rates).reshape(1, NX, NY, NZ)
    weights = quad_weight.astype(jnp.float32)
    weight_sum = jnp.sum(weights)
    head_list = []
    adjoint_list = []
    zone_gradient = jnp.zeros((NX // 4, NY // 4, NZ // 4), jnp.float32)
    for node_no in range(NODES):
        coarse_logk = log_conductivity(field_seeds[node_no], NX, NY, NZ, 0)
        operators = []
        for level_at in range(LEVELS):
            padded = jnp.pad(coarse_logk, ((1, 1), (0, 0), (0, 0)))
            operators.append(build_operator(padded, True, True, 0.25 ** level_at))
            if level_at + 1 < LEVELS:
                coarse_logk = restrict_all(coarse_logk)

        def coarse_fn(level_at, residue, operators=operators):
            return prolong_all(vcycle(level_at + 1, restrict_all(residue), operators, zero_pad,
                                      lambda lvl_at, res_now: coarse_fn(lvl_at, res_now, operators)))

        head_now = vcycle(0, source, operators, zero_pad, coarse_fn)[0]
        adjoint_now = vcycle(0, sensitivity[None], operators, zero_pad, coarse_fn)[0]
        head_list.append(head_now)
        adjoint_list.append(adjoint_now)
        cells = cell_gradient(operators[0], jnp.pad(head_now, ((1, 1), (0, 0), (0, 0))),
                              jnp.pad(adjoint_now, ((1, 1), (0, 0), (0, 0))), True, True)
        zone_gradient = zone_gradient + (weights[node_no] / weight_sum) * zone_total(cells)
    return jnp.stack(head_list), jnp.stack(adjoint_list), zone_gradient
```

```python
import functools

import jax
import jax.numpy as jnp
from jax import lax
from jax.experimental import pallas as pl
from jax.experimental.pallas import tpu as pltpu
from jax.sharding import PartitionSpec as P

LEVELS = 5
SWEEPS = 2
COARSE_SWEEPS = 8
OMEGA = 0.8
REACH = 3

F32 = jnp.float32


def iota(shape, axis):
    return lax.broadcasted_iota(jnp.int32, shape, axis)


def pairing(rows, cols, row_shift, col_shift, dtype):
    shape = (rows, cols)
    same = jnp.right_shift(iota(shape, 0), row_shift) == jnp.right_shift(iota(shape, 1), col_shift)
    return jnp.where(same, 1.0, 0.0).astype(dtype)


def split(x, terms):
    parts = []
    for _ in range(terms):
        part = x.astype(jnp.bfloat16)
        parts.append(part)
        x = x - part.astype(F32)
    return parts


def right_mul(x, cols, row_shift, col_shift, terms):
    m = pairing(x.shape[1], cols, row_shift, col_shift, jnp.bfloat16)
    out = None
    for part in split(x, terms):
        y = jnp.dot(part, m, preferred_element_type=F32)
        out = y if out is None else out + y
    return out


def left_mul(x, rows, row_shift, col_shift, terms):
    if x.shape[0] < 16 or rows < 16:
        m = pairing(rows, x.shape[0], row_shift, col_shift, F32)
        return jnp.dot(m, x, precision=lax.Precision.HIGHEST, preferred_element_type=F32)
    m = pairing(rows, x.shape[0], row_shift, col_shift, jnp.bfloat16)
    out = None
    for part in split(x, terms):
        y = jnp.dot(m, part, preferred_element_type=F32)
        out = y if out is None else out + y
    return out


def restrict2(x, shape, terms=2):
    return left_mul(right_mul(x, shape[1], 1, 0, terms), shape[0], 0, 1, terms)


def prolong2(x, shape, terms=2):
    return right_mul(left_mul(x, shape[0], 1, 0, terms), shape[1], 0, 1, terms)


def roll(x, shift, axis):
    return pltpu.roll(x, shift % x.shape[axis], axis)


def nsum(x, size):
    iy, iz = iota(x.shape, 0), iota(x.shape, 1)
    total = jnp.where(iy > 0, roll(x, 1, 0), 0.0)
    total = total + jnp.where(iy < size[0] - 1, roll(x, -1, 0), 0.0)
    total = total + jnp.where(iz > 0, roll(x, 1, 1), 0.0)
    return total + jnp.where(iz < size[1] - 1, roll(x, -1, 1), 0.0)


def each(start, stop, fn):
    def step(p, carry):
        fn(p)
        return carry

    if isinstance(start, int) and isinstance(stop, int) and stop - start <= 2:
        for p in range(start, stop):
            fn(p)
        return
    lax.fori_loop(start, stop, step, 0)


def both(fn):
    for f in range(2):
        fn(f)


def diag_plane(center, below, above, x_now, x_last, size):
    iy = iota(center.shape, 0)
    d = below + above + nsum(center, size)
    outside = jnp.where(iy == 0, 2.0, 0.0) + jnp.where(iy == size[0] - 1, 2.0, 0.0)
    ends = jnp.where(x_now == 0, 2.0, 0.0) + jnp.where(x_now == x_last, 2.0, 0.0)
    return d + (outside + ends) * center


def inside(shape, size, x_now, x_last):
    ok = (iota(shape, 0) < size[0]) & (iota(shape, 1) < size[1])
    return ok & ((x_now >= 0) & (x_now <= x_last))


def kernel(ns, sizes, pads, seed_ref, weight_ref, recharge_ref, cells_ref, rates_ref, sens_ref,
           head_ref, adj_ref, zone_ref,
           b0, e0, d0, q0, g0, c0, ua, ub, l0, ie0, pv0,
           b1, l1, e1, ie1, d1, q1, g1, c1, va, vb, pv1,
           l2, b2, *rest):
    coarse = [rest[8 * i: 8 * i + 8] for i in range(3)]
    own_zone, other_zone = rest[24:26]
    s_halo, r_halo, s_l1, r_l1, s_b1, r_b1, s_l2, r_l2, s_b2, r_b2, s_z, r_z = rest[26:]
    me = lax.axis_index("slab")
    node = lax.axis_index("node")
    size0, size1, size2 = sizes[:3]
    pad1, pad2 = pads[1], pads[2]
    cx = recharge_ref.shape[0]
    last0 = cx * ns - 1
    own1 = 2 * REACH
    last1 = 2 * ns - 1

    def remote(src, dst, send, recv, slab):
        return pltpu.make_async_remote_copy(
            src_ref=src, dst_ref=dst, send_sem=send, recv_sem=recv,
            device_id={"slab": slab}, device_id_type=pl.DeviceIdType.MESH)

    zero0 = jnp.zeros(size0, F32)
    zero1 = jnp.zeros(pad1, F32)

    @pl.when(me == 0)
    def _():
        each(0, cx, lambda p: both(lambda f: b0.__setitem__((f, p), zero0)))

    @pl.when(me == ns - 1)
    def _():
        each(2 * cx, 3 * cx, lambda p: both(lambda f: b0.__setitem__((f, p), zero0)))

    def clear1(p):
        l1[p] = zero1
        b1[0, p] = zero1
        b1[1, p] = zero1

    each(0, 2 * own1 + 2, clear1)

    barrier = pltpu.get_barrier_semaphore()

    def greet(k):
        peer = lax.rem(me + k, ns)
        pl.semaphore_signal(barrier, inc=1, device_id={"slab": peer},
                            device_id_type=pl.DeviceIdType.MESH)

    each(1, ns, greet)
    pl.semaphore_signal(barrier, inc=1, device_id={"node": 1 - node},
                        device_id_type=pl.DeviceIdType.MESH)

    place = iota(size0, 0) * size0[1] + iota(size0, 1)

    def sources(p):
        value = recharge_ref[p]
        here = place + p * (size0[0] * size0[1])
        for w in range(cells_ref.shape[0]):
            value = value + jnp.where(here == cells_ref[w], rates_ref[w], 0.0)
        b0[0, cx + p] = value
        b0[1, cx + p] = sens_ref[p]

    each(0, cx, sources)
    pl.semaphore_wait(barrier, ns)

    half = cx // 2
    halo = [(1, cx + half, half, 0), (-1, cx, 2 * cx, 1),
            (1, cx, 0, 2), (-1, cx + half, 2 * cx + half, 3)]

    def halo_copy(way, src, dst, i, slab):
        return remote(b0.at[:, pl.ds(src, half)], b0.at[:, pl.ds(dst, half)],
                      s_halo.at[i], r_halo.at[i], slab)

    def in_range(slab):
        return (slab >= 0) & (slab < ns)

    def halo_start(i):
        way = halo[i][0]

        @pl.when(in_range(me + way))
        def _():
            halo_copy(*halo[i], me + way).start()

    def halo_wait(i):
        way = halo[i][0]

        @pl.when(in_range(me - way))
        def _():
            halo_copy(*halo[i], me - way).wait_recv()

    for i in range(4):
        halo_start(i)

    def near_copy(ref, send, recv, lead, d, slab):
        src, dst = pl.ds(own1, 2), pl.ds(own1 - 2 * d, 2)
        index = (slice(None),) if lead else ()
        return remote(ref.at[index + (src,)], ref.at[index + (dst,)],
                      send.at[d + REACH], recv.at[d + REACH], slab)

    steps = [s * d for d in range(1, REACH + 1) for s in (1, -1)]

    def near_start(*args):
        for d in steps:
            @pl.when(in_range(me + d))
            def _():
                near_copy(*args, d, me + d).start()

    def near_wait(*args, distances):
        for d in steps:
            if abs(d) in distances:
                @pl.when(in_range(me - d))
                def _():
                    near_copy(*args, d, me - d).wait_recv()

    def near_sent(*args):
        for d in steps:
            @pl.when(in_range(me + d))
            def _():
                near_copy(*args, d, me + d).wait_send()

    def all_copy(ref, send, recv, lead, k, slab, owner):
        index = (slice(None),) if lead else ()
        at = ref.at[index + (pl.ds(owner, 1),)]
        return remote(at, at, send.at[k], recv.at[k], slab)

    def all_start(*args):
        each(1, ns, lambda k: all_copy(*args, k, lax.rem(me + k, ns), me).start())

    def all_wait(*args):
        def wait(k):
            peer = lax.rem(me - k + ns, ns)
            all_copy(*args, k, peer, peer).wait_recv()

        each(1, ns, wait)

    def all_sent(*args):
        each(1, ns, lambda k: all_copy(*args, k, lax.rem(me + k, ns), me).wait_send())

    seed_part = seed_ref[0] * 277803737 + 1013904223
    hashed_place = place * 747796405
    first0 = me * cx - cx

    def logk_plane(p):
        x_now = first0 - 1 + p
        q = hashed_place + (x_now * (size0[0] * size0[1]) * 747796405 + seed_part)
        q = jnp.bitwise_xor(q, lax.shift_right_logical(q, jnp.full(size0, 15, jnp.int32)))
        q = q * 1274126177
        q = jnp.bitwise_xor(q, lax.shift_right_logical(q, jnp.full(size0, 13, jnp.int32)))
        low = jnp.bitwise_and(q, 65535)
        logk = 3.0 * (low.astype(F32) / 65536.0) - 1.5
        l0[p] = logk
        known = (x_now >= 0) & (x_now <= last0)
        e0[p] = jnp.where(known, jnp.exp(0.5 * logk), 0.0)
        ie0[p] = jnp.exp(-0.5 * logk)

    each(0, 3 * cx + 2, logk_plane)
    for i in range(2):
        pair = l0[cx + 1 + 2 * i] + l0[cx + 2 + 2 * i]
        l1[own1 + i] = restrict2(pair, pad1, 3) * 0.125
    near_start(l1, s_l1, r_l1, False)
    l2[pl.ds(me, 1)] = (restrict2(l1[own1] + l1[own1 + 1], pad2, 3) * 0.125)[None]
    all_start(l2, s_l2, r_l2, False)

    def operator0(p):
        x_now = first0 + p
        center = e0[p + 1]
        d = diag_plane(center, e0[p], e0[p + 2], x_now, last0, size0)
        known = (x_now >= 0) & (x_now <= last0)
        q = jnp.where(known, OMEGA / d, 0.0)
        d0[p] = d
        q0[p] = q
        g0[p] = q * center

    each(0, 3 * cx, operator0)

    def first0_c(p):
        q = q0[p]
        c0[0, p] = q * b0[0, p]
        c0[1, p] = q * b0[1, p]

    def first_sweeps(u, c, g, size, p):
        gain = g[p]

        def one(f):
            now = c[f, p]
            total = c[f, p - 1] + c[f, p + 1] + nsum(now, size)
            u[f, p] = (2.0 - OMEGA) * now + gain * total

        both(one)

    def sweep(u, c, g, out, size, p, gp=None, cp=None):
        gp = p if gp is None else gp
        cp = p if cp is None else cp
        gain = g[gp]

        def one(f):
            now = u[f, p]
            total = u[f, p - 1] + u[f, p + 1] + nsum(now, size)
            out[f, p] = (1.0 - OMEGA) * now + c[f, cp] + gain * total

        both(one)

    def residue(u, b, e, d, size, f, p, ep, dp, bp):
        now = u[f, p]
        total = u[f, p - 1] + u[f, p + 1] + nsum(now, size)
        return b[f, bp] + e[ep] * total - d[dp] * now

    each(cx, 2 * cx, first0_c)

    near_wait(l1, s_l1, r_l1, False, distances=(1, 2, 3))
    first1 = 2 * me - own1
    width1 = 2 * own1 + 2

    def exp1(p):
        x_now = first1 + p
        ok = inside(pad1, size1, x_now, last1)
        logk = l1[p]
        e1[p] = jnp.where(ok, jnp.exp(0.5 * logk), 0.0)
        ie1[p] = jnp.where(ok, jnp.exp(-0.5 * logk), 0.0)

    each(0, width1, exp1)

    def operator1(p):
        x_now = first1 + p
        center = e1[p]
        d = diag_plane(center, e1[p - 1], e1[p + 1], x_now, last1, size1)
        q = jnp.where(inside(pad1, size1, x_now, last1), OMEGA / d, 0.0)
        d1[p] = d
        q1[p] = q
        g1[p] = q * center

    each(1, width1 - 1, operator1)

    halo_wait(0)
    halo_wait(1)
    each(half, cx, first0_c)
    each(2 * cx, 2 * cx + half, first0_c)
    each(cx - 1, 2 * cx + 1, functools.partial(first_sweeps, ua, c0, g0, size0))

    for f in range(2):
        for i in range(2):
            p = cx + 2 * i
            pair = (residue(ua, b0, e0, d0, size0, f, p, p + 1, p, p)
                    + residue(ua, b0, e0, d0, size0, f, p + 1, p + 2, p + 1, p + 1))
            b1[f, own1 + i] = restrict2(pair, pad1) * 0.5
    near_start(b1, s_b1, r_b1, True)

    all_wait(l2, s_l2, r_l2, False)
    counts = [ns >> i for i in range(3)]
    logs = l2
    for i in range(3):
        e, ie, d, q, g, c, u, w = coarse[i]
        size, pad, n = sizes[2 + i], pads[2 + i], counts[i]
        e[0] = jnp.zeros(pad, F32)
        e[n + 1] = jnp.zeros(pad, F32)
        for ref in (u, w):
            for f in range(2):
                ref[f, 0] = jnp.zeros(pad, F32)
                ref[f, n + 1] = jnp.zeros(pad, F32)
        source = l2 if i == 0 else None

        def exps(p, e=e, ie=ie, size=size, pad=pad, n=n, i=i, d=d):
            if i == 0:
                logk = l2[p]
            else:
                above = coarse[i - 1][4] if i > 1 else l2
                logk = restrict2(above[2 * p] + above[2 * p + 1], pad, 3) * 0.125
                g_now = coarse[i][4]
                g_now[p] = logk
            ok = inside(pad, size, p, n - 1)
            e[p + 1] = jnp.where(ok, jnp.exp(0.5 * logk), 0.0)
            ie[p] = jnp.where(ok, jnp.exp(-0.5 * logk), 0.0)

        each(0, n, exps)
    for i in range(3):
        e, ie, d, q, g, c, u, w = coarse[i]
        size, pad, n = sizes[2 + i], pads[2 + i], counts[i]

        def ops(p, e=e, d=d, q=q, g=g, size=size, pad=pad, n=n):
            center = e[p + 1]
            dd = diag_plane(center, e[p], e[p + 2], p, n - 1, size)
            qq = jnp.where(inside(pad, size, p, n - 1), OMEGA / dd, 0.0)
            d[p] = dd
            q[p] = qq
            g[p] = qq * center

        each(0, n, ops)

    def first1_c(p):
        q = q1[p]
        c1[0, p] = q * b1[0, p]
        c1[1, p] = q * b1[1, p]

    near_wait(b1, s_b1, r_b1, True, distances=(1,))
    each(own1 - 2, own1 + 4, first1_c)
    each(own1 - 1, own1 + 3, functools.partial(first_sweeps, va, c1, g1, size1))
    for f in range(2):
        pair = (residue(va, b1, e1, d1, size1, f, own1, own1, own1, own1)
                + residue(va, b1, e1, d1, size1, f, own1 + 1, own1 + 1, own1 + 1, own1 + 1))
        b2[f, pl.ds(me, 1)] = (restrict2(pair, pad2) * 0.5)[None]
    all_start(b2, s_b2, r_b2, True)

    halo_wait(2)
    halo_wait(3)
    each(0, half, first0_c)
    each(2 * cx + half, 3 * cx, first0_c)
    each(1, cx - 1, functools.partial(first_sweeps, ua, c0, g0, size0))
    each(2 * cx + 1, 3 * cx - 1, functools.partial(first_sweeps, ua, c0, g0, size0))
    near_wait(b1, s_b1, r_b1, True, distances=(2, 3))
    each(own1 - 5, own1 - 2, first1_c)
    each(own1 + 4, own1 + 7, first1_c)
    each(own1 - 4, own1 - 1, functools.partial(first_sweeps, va, c1, g1, size1))
    each(own1 + 3, own1 + 6, functools.partial(first_sweeps, va, c1, g1, size1))

    all_wait(b2, s_b2, r_b2, True)

    def solve(i, source):
        e, ie, d, q, g, c, u, w = coarse[i]
        size, pad, n = sizes[2 + i], pads[2 + i], counts[i]

        def begin(p):
            def one(f):
                value = q[p] * source[f, p]
                c[f, p] = value
                u[f, p + 1] = value

            both(one)

        each(0, n, begin)

        def full(src, dst):
            each(1, n + 1, lambda p: sweep(src, c, g, dst, size, p, p - 1, p - 1))

        if i == 2:
            now, then = u, w
            for _ in range(COARSE_SWEEPS - 1):
                full(now, then)
                now, then = then, now
            return now
        full(u, w)
        below = rest_source[i + 1]

        def down(p):
            def one(f):
                pair = (residue(w, source, e, d, size, f, 2 * p + 1, 2 * p + 1, 2 * p, 2 * p)
                        + residue(w, source, e, d, size, f, 2 * p + 2, 2 * p + 2, 2 * p + 1, 2 * p + 1))
                below[f, p] = restrict2(pair, pads[3 + i]) * 0.5

            both(one)

        each(0, counts[i + 1], down)
        fix = solve(i + 1, below)
        fix_inv = coarse[i + 1][1]

        def up(p):
            def one(f):
                add = prolong2(fix[f, p + 1] * fix_inv[p], pad)
                w[f, 2 * p + 1] = w[f, 2 * p + 1] + e[2 * p + 1] * add
                w[f, 2 * p + 2] = w[f, 2 * p + 2] + e[2 * p + 2] * add

            both(one)

        each(0, counts[i + 1], up)
        full(w, u)
        full(u, w)
        return w

    rest_source = [b2, coarse[1][6], coarse[2][6]]
    rest_source = [b2, pv0, pv1]
    top = solve(0, b2)
    top_inv = coarse[0][1]

    def correct1(k):
        at = jnp.clip(me - 2 + k, 0, ns - 1)
        p = own1 - 4 + 2 * k

        def one(f):
            add = prolong2(top[f, at + 1] * top_inv[at], pad1)
            va[f, p] = va[f, p] + e1[p] * add
            va[f, p + 1] = va[f, p + 1] + e1[p + 1] * add

        both(one)

    each(0, 5, correct1)
    each(own1 - 3, own1 + 5, functools.partial(sweep, va, c1, g1, vb, size1))
    each(own1 - 2, own1 + 4, functools.partial(sweep, vb, c1, g1, va, size1))

    def correct0(f, l, planes):
        add = prolong2(va[f, l] * ie1[l], size0)
        for p in planes:
            ua[f, p] = ua[f, p] + e0[p + 1] * add

    for f in range(2):
        correct0(f, own1 - 2, (1,))
        correct0(f, own1 + 3, (3 * cx - 2,))

    def middle(k):
        p = 2 + 2 * k
        both(lambda f: correct0(f, own1 - 1 + k, (p, p + 1)))

    each(0, 4, middle)
    each(2, 3 * cx - 2, functools.partial(sweep, ua, c0, g0, ub, size0))
    each(3, 3 * cx - 3, functools.partial(sweep, ub, c0, g0, ua, size0))

    def heads(p):
        inv = ie0[p + 1]
        ub[0, p] = ua[0, p] * inv
        ub[1, p] = ua[1, p] * inv

    each(cx - 1, 2 * cx + 1, heads)

    iy, iz = iota(size0, 0), iota(size0, 1)
    y_end = (iy == 0) | (iy == size0[0] - 1)

    def gradient(p, carry):
        plain, by_y, by_z = carry
        h, a, e = ub[0, p], ub[1, p], e0[p + 1]
        head_ref[0, p - cx] = h
        adj_ref[0, p - cx] = a
        lower = e * e0[p] * (h - ub[0, p - 1]) * (a - ub[1, p - 1])
        upper = e * e0[p + 2] * (h - ub[0, p + 1]) * (a - ub[1, p + 1])
        x_now = first0 + p
        edge = 2.0 * ua[0, p] * ua[1, p]
        ends = jnp.where(x_now == 0, 1.0, 0.0) + jnp.where(x_now == last0, 1.0, 0.0)
        plain = plain + 0.5 * (lower + upper) + edge * (ends + jnp.where(y_end, 1.0, 0.0))
        by_y = by_y + e * roll(e, 1, 0) * (h - roll(h, 1, 0)) * (a - roll(a, 1, 0))
        by_z = by_z + e * roll(e, 1, 1) * (h - roll(h, 1, 1)) * (a - roll(a, 1, 1))
        return plain, by_y, by_z

    plain, by_y, by_z = lax.fori_loop(cx, 2 * cx, gradient, (zero0, zero0, zero0))
    by_y = jnp.where(iy > 0, by_y, 0.0)
    by_z = jnp.where(iz > 0, by_z, 0.0)
    cells = plain + 0.5 * (by_y + roll(by_y, -1, 0) + by_z + roll(by_z, -1, 1))
    zy, zz = zone_ref.shape[1:]
    zone = right_mul(left_mul(cells, zy, 0, 2, 3), zz, 2, 0, 3)
    weight_sum = weight_ref[0]
    for w in range(1, weight_ref.shape[0]):
        weight_sum = weight_sum + weight_ref[w]
    own = jnp.full(zone.shape, weight_ref[node], jnp.int32).astype(F32)
    portion = own / jnp.full(zone.shape, weight_sum, jnp.int32).astype(F32)
    own_zone[...] = -(portion * zone)
    zone_copy = pltpu.make_async_remote_copy(
        src_ref=own_zone, dst_ref=other_zone, send_sem=s_z, recv_sem=r_z,
        device_id={"node": 1 - node}, device_id_type=pl.DeviceIdType.MESH)
    zone_copy.start()

    for i in range(4):
        way = halo[i][0]

        @pl.when(in_range(me + way))
        def _():
            halo_copy(*halo[i], me + way).wait_send()

    near_sent(l1, s_l1, r_l1, False)
    near_sent(b1, s_b1, r_b1, True)
    all_sent(l2, s_l2, r_l2, False)
    all_sent(b2, s_b2, r_b2, True)
    zone_copy.wait()
    zone_ref[0] = own_zone[...] + other_zone[...]


def body(ns, field_seeds, quad_weight, recharge, well_cells, well_rates, sensitivity):
    cx, ny, nz = recharge.shape
    sizes = [(ny >> l, nz >> l) for l in range(LEVELS)]
    pads = [(max(y, 8), max(z, 128)) for y, z in sizes]
    wide = 3 * cx
    near = 4 * REACH + 2
    vmem, smem = pltpu.VMEM, pltpu.SMEM
    p0, p1, p2 = pads[:3]
    dma = pltpu.SemaphoreType.DMA
    scratch = [
        vmem((2, wide) + p0, F32), vmem((wide + 2,) + p0, F32), vmem((wide,) + p0, F32),
        vmem((wide,) + p0, F32), vmem((wide,) + p0, F32), vmem((2, wide) + p0, F32),
        vmem((2, wide) + p0, F32), vmem((2, wide) + p0, F32), vmem((wide + 2,) + p0, F32),
        vmem((wide + 2,) + p0, F32), vmem((2, ns // 2) + pads[3], F32),
        vmem((2, near) + p1, F32), vmem((near,) + p1, F32), vmem((near,) + p1, F32),
        vmem((near,) + p1, F32), vmem((near,) + p1, F32), vmem((near,) + p1, F32),
        vmem((near,) + p1, F32), vmem((2, near) + p1, F32), vmem((2, near) + p1, F32),
        vmem((2, near) + p1, F32), vmem((2, ns // 4) + pads[4], F32),
        vmem((ns,) + p2, F32), vmem((2, ns) + p2, F32),
    ]
    for i in range(3):
        n, pad = ns >> i, pads[2 + i]
        scratch += [vmem((n + 2,) + pad, F32), vmem((n,) + pad, F32), vmem((n,) + pad, F32),
                    vmem((n,) + pad, F32), vmem((n,) + pad, F32), vmem((2, n) + pad, F32),
                    vmem((2, n + 2) + pad, F32), vmem((2, n + 2) + pad, F32)]
    zone = (ny // 4, nz // 4)
    scratch += [vmem(zone, F32), vmem(zone, F32)]
    spread = 2 * REACH + 1
    scratch += [dma((4,)), dma((4,)), dma((spread,)), dma((spread,)), dma((spread,)), dma((spread,)),
                dma((ns,)), dma((ns,)), dma((ns,)), dma((ns,)), dma, dma]
    in_v, in_s = pl.BlockSpec(memory_space=vmem), pl.BlockSpec(memory_space=smem)
    field = jax.ShapeDtypeStruct((1, cx, ny, nz), F32)
    return pl.pallas_call(
        functools.partial(kernel, ns, sizes, pads),
        out_shape=(field, field, jax.ShapeDtypeStruct((1,) + zone, F32)),
        in_specs=[in_s, in_s, in_v, in_s, in_s, in_v],
        out_specs=(in_v, in_v, in_v),
        scratch_shapes=scratch,
        compiler_params=pltpu.CompilerParams(
            collective_id=0, has_side_effects=True, vmem_limit_bytes=48 * 1024 * 1024),
    )(field_seeds, quad_weight, recharge, well_cells, well_rates, sensitivity)


def solution(mesh):
    placed = (
        P(("groups", "node")),
        P("groups"),
        P(("groups", "slab"), None, None),
        P(("groups", "slab")),
        P(("groups", "slab")),
        P(("groups", "slab"), None, None),
    )
    return jax.shard_map(
        functools.partial(body, mesh.shape["slab"]),
        mesh=mesh,
        in_specs=placed,
        out_specs=(
            P(("groups", "node"), "slab", None, None),
            P(("groups", "node"), "slab", None, None),
            P(("groups", "slab"), None, None),
        ),
        check_vma=False,
    )
```

```python
import functools

import jax
import jax.numpy as jnp
from jax import lax
from jax.experimental import pallas as pl
from jax.experimental.pallas import tpu as pltpu
from jax.sharding import PartitionSpec as P

LEVELS = 5
SWEEPS = 2
COARSE_SWEEPS = 8
OMEGA = 0.8
REACH = 3

F32 = jnp.float32


def iota(shape, axis):
    return lax.broadcasted_iota(jnp.int32, shape, axis)


def matrix(rows, cols, rule, dtype=jnp.bfloat16):
    shape = (rows, cols)
    return jnp.where(rule(iota(shape, 0), iota(shape, 1)), 1.0, 0.0).astype(dtype)


def half_of(i):
    return jnp.right_shift(i, 1)


def coarsen(i, j):
    return half_of(i) == j


def refine(i, j):
    return i == half_of(j)


def split(x, terms):
    parts = []
    for _ in range(terms):
        part = x.astype(jnp.bfloat16)
        parts.append(part)
        x = x - part.astype(F32)
    return parts


def right_mul(x, cols, rule, terms=2):
    m = matrix(x.shape[1], cols, rule)
    out = None
    for part in split(x, terms):
        y = jnp.dot(part, m, preferred_element_type=F32)
        out = y if out is None else out + y
    return out


def left_mul(x, rows, rule, terms=2):
    m = matrix(rows, x.shape[0], lambda i, j: rule(j, i))
    out = None
    for part in split(x, terms):
        y = jnp.dot(m, part, preferred_element_type=F32)
        out = y if out is None else out + y
    return out


def restrict2(x, shape, terms=2):
    return left_mul(right_mul(x, shape[1], coarsen, terms), shape[0], coarsen, terms)


def prolong2(x, shape, terms=2):
    return right_mul(left_mul(x, shape[0], refine, terms), shape[1], refine, terms)


def roll(x, shift, axis):
    return pltpu.roll(x, shift % x.shape[axis], axis)


def nsum(x, size, fields=1):
    iy, iz = iota(x.shape, 0), iota(x.shape, 1)
    if fields > 1:
        iz = jnp.bitwise_and(iz, size[1] - 1)
    total = jnp.where(iy > 0, roll(x, 1, 0), 0.0)
    total = total + jnp.where(iy < size[0] - 1, roll(x, -1, 0), 0.0)
    total = total + jnp.where(iz > 0, roll(x, 1, 1), 0.0)
    return total + jnp.where(iz < size[1] - 1, roll(x, -1, 1), 0.0)


def each(start, stop, fn, unroll=2):
    def step(p, carry):
        fn(p)
        return carry

    if stop - start <= unroll:
        for p in range(start, stop):
            fn(p)
        return
    lax.fori_loop(start, stop, step, 0)


def both(fn):
    for f in range(2):
        fn(f)


def diag_plane(center, below, above, x_now, x_last, size, fields=1):
    iy = iota(center.shape, 0)
    d = below + above + nsum(center, size, fields)
    outside = jnp.where(iy == 0, 2.0, 0.0) + jnp.where(iy == size[0] - 1, 2.0, 0.0)
    ends = jnp.where(x_now == 0, 2.0, 0.0) + jnp.where(x_now == x_last, 2.0, 0.0)
    return d + (outside + ends) * center


def inside(shape, size, x_now, x_last, fields=1):
    ok = (iota(shape, 0) < size[0]) & (iota(shape, 1) < fields * size[1])
    return ok & ((x_now >= 0) & (x_now <= x_last))


def kernel(ns, sizes, pads, seed_ref, weight_ref, recharge_ref, cells_ref, rates_ref, sens_ref,
           head_ref, adj_ref, zone_ref,
           b0, e0, d0, q0, g0, c0, ua, ub, l0, ie0, b3,
           b1, l1, e1, ie1, d1, q1, g1, c1, va, vb, b4,
           l2, b2, *rest):
    coarse = [rest[8 * i: 8 * i + 8] for i in range(3)]
    own_zone, other_zone = rest[24:26]
    s_halo, r_halo, s_in, s_l1, r_l1, s_b1, r_b1, s_l2, r_l2, s_b2, r_b2, s_z, r_z = rest[26:]
    me = lax.axis_index("slab")
    node = lax.axis_index("node")
    size0, size1, size2 = sizes[:3]
    pad1, pad2 = pads[1], pads[2]
    cx = recharge_ref.shape[0]
    last0 = cx * ns - 1
    own1 = 2 * REACH
    last1 = 2 * ns - 1

    def remote(src, dst, send, recv, slab):
        return pltpu.make_async_remote_copy(
            src_ref=src, dst_ref=dst, send_sem=send, recv_sem=recv,
            device_id={"slab": slab}, device_id_type=pl.DeviceIdType.MESH)

    zero0 = jnp.zeros(size0, F32)
    zero1 = jnp.zeros(pad1, F32)

    @pl.when(me == 0)
    def _():
        each(0, cx, lambda p: both(lambda f: b0.__setitem__((f, p), zero0)))

    @pl.when(me == ns - 1)
    def _():
        each(2 * cx, 3 * cx, lambda p: both(lambda f: b0.__setitem__((f, p), zero0)))

    def clear1(p):
        l1[p] = zero1
        b1[0, p] = zero1
        b1[1, p] = zero1

    each(0, 2 * own1 + 2, clear1)

    barrier = pltpu.get_barrier_semaphore()

    def greet(k):
        peer = lax.rem(me + k, ns)
        pl.semaphore_signal(barrier, inc=1, device_id={"slab": peer},
                            device_id_type=pl.DeviceIdType.MESH)

    each(1, ns, greet)
    pl.semaphore_signal(barrier, inc=1, device_id={"node": 1 - node},
                        device_id_type=pl.DeviceIdType.MESH)

    loads = [pltpu.make_async_copy(ref, b0.at[f, pl.ds(cx, cx)], s_in.at[f])
             for f, ref in enumerate((recharge_ref, sens_ref))]
    for load in loads:
        load.start()

    place = iota(size0, 0) * size0[1] + iota(size0, 1)

    def sources(p):
        value = b0[0, cx + p]
        here = place + p * (size0[0] * size0[1])
        for w in range(cells_ref.shape[0]):
            value = value + jnp.where(here == cells_ref[w], rates_ref[w], 0.0)
        b0[0, cx + p] = value

    for load in loads:
        load.wait()
    each(0, cx, sources)
    pl.semaphore_wait(barrier, ns)

    half = cx // 2
    halo = [(1, cx + half, half, 0), (-1, cx, 2 * cx, 1),
            (1, cx, 0, 2), (-1, cx + half, 2 * cx + half, 3)]

    def halo_copy(way, src, dst, i, slab):
        field = pl.ds(node, 1)
        return remote(b0.at[field, pl.ds(src, half)], b0.at[field, pl.ds(dst, half)],
                      s_halo.at[i], r_halo.at[i], slab)

    def pass_copy(way, src, dst, i, slab, field):
        at = b0.at[pl.ds(field, 1), pl.ds(dst, half)]
        return pltpu.make_async_remote_copy(
            src_ref=at, dst_ref=at, send_sem=s_halo.at[4 + i], recv_sem=r_halo.at[4 + i],
            device_id={"node": 1 - node}, device_id_type=pl.DeviceIdType.MESH)

    def in_range(slab):
        return (slab >= 0) & (slab < ns)

    def halo_start(i):
        way = halo[i][0]

        @pl.when(in_range(me + way))
        def _():
            halo_copy(*halo[i], me + way).start()

    def halo_pass(i):
        way = halo[i][0]

        @pl.when(in_range(me - way))
        def _():
            halo_copy(*halo[i], me - way).wait_recv()
            pass_copy(*halo[i], me, node).start()

    def halo_wait(i):
        way = halo[i][0]

        @pl.when(in_range(me - way))
        def _():
            pass_copy(*halo[i], me, 1 - node).wait_recv()

    def halo_sent(i):
        way = halo[i][0]

        @pl.when(in_range(me + way))
        def _():
            halo_copy(*halo[i], me + way).wait_send()

        @pl.when(in_range(me - way))
        def _():
            pass_copy(*halo[i], me, node).wait_send()

    for i in range(2):
        halo_start(i)

    def near_copy(ref, send, recv, lead, d, slab):
        src, dst = pl.ds(own1, 2), pl.ds(own1 - 2 * d, 2)
        index = (slice(None),) if lead else ()
        return remote(ref.at[index + (src,)], ref.at[index + (dst,)],
                      send.at[d + REACH], recv.at[d + REACH], slab)

    steps = [s * d for d in range(1, REACH + 1) for s in (1, -1)]

    def near_start(*args):
        for d in steps:
            @pl.when(in_range(me + d))
            def _():
                near_copy(*args, d, me + d).start()

    def near_wait(*args, distances):
        for d in steps:
            if abs(d) in distances:
                @pl.when(in_range(me - d))
                def _():
                    near_copy(*args, d, me - d).wait_recv()

    def near_sent(*args):
        for d in steps:
            @pl.when(in_range(me + d))
            def _():
                near_copy(*args, d, me + d).wait_send()

    def all_copy(ref, send, recv, lead, k, slab, owner):
        index = (slice(None),) if lead else ()
        at = ref.at[index + (pl.ds(owner, 1),)]
        return remote(at, at, send.at[k], recv.at[k], slab)

    def all_start(*args):
        each(1, ns, lambda k: all_copy(*args, k, lax.rem(me + k, ns), me).start())

    def all_wait(*args):
        def wait(k):
            peer = lax.rem(me - k + ns, ns)
            all_copy(*args, k, peer, peer).wait_recv()

        each(1, ns, wait)

    def all_sent(*args):
        each(1, ns, lambda k: all_copy(*args, k, lax.rem(me + k, ns), me).wait_send())

    seed_part = seed_ref[0] * 277803737 + 1013904223
    hashed_place = place * 747796405
    first0 = me * cx - cx

    def logk_plane(p):
        x_now = first0 - 1 + p
        q = hashed_place + (x_now * (size0[0] * size0[1]) * 747796405 + seed_part)
        q = jnp.bitwise_xor(q, lax.shift_right_logical(q, jnp.full(size0, 15, jnp.int32)))
        q = q * 1274126177
        q = jnp.bitwise_xor(q, lax.shift_right_logical(q, jnp.full(size0, 13, jnp.int32)))
        low = jnp.bitwise_and(q, 65535)
        logk = 3.0 * (low.astype(F32) / 65536.0) - 1.5
        l0[p] = logk
        known = (x_now >= 0) & (x_now <= last0)
        e0[p] = jnp.where(known, jnp.exp(0.5 * logk), 0.0)
        ie0[p] = jnp.exp(-0.5 * logk)

    each(0, 3 * cx + 2, logk_plane)
    for i in range(2):
        pair = l0[cx + 1 + 2 * i] + l0[cx + 2 + 2 * i]
        l1[own1 + i] = restrict2(pair, pad1, 3) * 0.125
    near_start(l1, s_l1, r_l1, False)
    both_fields = right_mul(l1[own1] + l1[own1 + 1], pad2[1],
                            lambda i, j: half_of(i) == jnp.bitwise_and(j, size2[1] - 1), 3)
    l2[pl.ds(me, 1)] = (left_mul(both_fields, pad2[0], coarsen, 3) * 0.125)[None]
    all_start(l2, s_l2, r_l2, False)

    def operator0(p):
        x_now = first0 + p
        center = e0[p + 1]
        d = diag_plane(center, e0[p], e0[p + 2], x_now, last0, size0)
        known = (x_now >= 0) & (x_now <= last0)
        q = jnp.where(known, OMEGA / d, 0.0)
        d0[p] = d
        q0[p] = q
        g0[p] = q * center

    each(0, 3 * cx, operator0)

    def first0_c(p):
        q = q0[p]
        c0[0, p] = q * b0[0, p]
        c0[1, p] = q * b0[1, p]

    def first_sweeps(u, c, g, size, p):
        gain = g[p]

        def one(f):
            now = c[f, p]
            total = c[f, p - 1] + c[f, p + 1] + nsum(now, size)
            u[f, p] = (2.0 - OMEGA) * now + gain * total

        both(one)

    def sweep(u, c, g, out, size, p, gp=None, cp=None):
        gp = p if gp is None else gp
        cp = p if cp is None else cp
        gain = g[gp]

        def one(f):
            now = u[f, p]
            total = u[f, p - 1] + u[f, p + 1] + nsum(now, size)
            out[f, p] = (1.0 - OMEGA) * now + c[f, cp] + gain * total

        both(one)

    def residue(u, b, e, d, size, f, p, ep, dp, bp):
        now = u[f, p]
        total = u[f, p - 1] + u[f, p + 1] + nsum(now, size)
        return b[f, bp] + e[ep] * total - d[dp] * now

    each(cx, 2 * cx, first0_c)

    halo_pass(0)
    halo_pass(1)
    halo_wait(0)
    halo_wait(1)
    each(half, cx, first0_c)
    each(2 * cx, 2 * cx + half, first0_c)
    each(cx - 1, 2 * cx + 1, functools.partial(first_sweeps, ua, c0, g0, size0))

    for f in range(2):
        for i in range(2):
            p = cx + 2 * i
            pair = (residue(ua, b0, e0, d0, size0, f, p, p + 1, p, p)
                    + residue(ua, b0, e0, d0, size0, f, p + 1, p + 2, p + 1, p + 1))
            b1[f, own1 + i] = restrict2(pair, pad1) * 0.5
    near_start(b1, s_b1, r_b1, True)

    near_wait(l1, s_l1, r_l1, False, distances=(1, 2, 3))
    first1 = 2 * me - own1
    width1 = 2 * own1 + 2

    def exp1(p):
        x_now = first1 + p
        ok = inside(pad1, size1, x_now, last1)
        logk = l1[p]
        e1[p] = jnp.where(ok, jnp.exp(0.5 * logk), 0.0)
        ie1[p] = jnp.where(ok, jnp.exp(-0.5 * logk), 0.0)

    each(0, width1, exp1)

    def operator1(p):
        x_now = first1 + p
        center = e1[p]
        d = diag_plane(center, e1[p - 1], e1[p + 1], x_now, last1, size1)
        q = jnp.where(inside(pad1, size1, x_now, last1), OMEGA / d, 0.0)
        d1[p] = d
        q1[p] = q
        g1[p] = q * center

    each(1, width1 - 1, operator1)

    all_wait(l2, s_l2, r_l2, False)
    counts = [ns >> i for i in range(3)]
    for i in range(3):
        e, ie, d, q, g, c, u, w = coarse[i]
        size, pad, n = sizes[2 + i], pads[2 + i], counts[i]
        e[0] = jnp.zeros(pad, F32)
        e[n + 1] = jnp.zeros(pad, F32)
        for ref in (u, w):
            ref[0] = jnp.zeros(pad, F32)
            ref[n + 1] = jnp.zeros(pad, F32)

        def exps(p, e=e, ie=ie, size=size, pad=pad, n=n, i=i, d=d):
            if i == 0:
                logk = l2[p]
            else:
                above = coarse[i - 1][4] if i > 1 else l2
                logk = restrict2(above[2 * p] + above[2 * p + 1], pad, 3) * 0.125
                g_now = coarse[i][4]
                g_now[p] = logk
            ok = inside(pad, size, p, n - 1, 2)
            e[p + 1] = jnp.where(ok, jnp.exp(0.5 * logk), 0.0)
            ie[p] = jnp.where(ok, jnp.exp(-0.5 * logk), 0.0)

        each(0, n, exps)
    for i in range(3):
        e, ie, d, q, g, c, u, w = coarse[i]
        size, pad, n = sizes[2 + i], pads[2 + i], counts[i]

        def ops(p, e=e, d=d, q=q, g=g, size=size, pad=pad, n=n):
            center = e[p + 1]
            dd = diag_plane(center, e[p], e[p + 2], p, n - 1, size, 2)
            qq = jnp.where(inside(pad, size, p, n - 1, 2), OMEGA / dd, 0.0)
            d[p] = dd
            q[p] = qq
            g[p] = qq * center

        each(0, n, ops)

    def first1_c(p):
        q = q1[p]
        c1[0, p] = q * b1[0, p]
        c1[1, p] = q * b1[1, p]

    near_wait(b1, s_b1, r_b1, True, distances=(1,))
    each(own1 - 2, own1 + 4, first1_c)
    each(own1 - 1, own1 + 3, functools.partial(first_sweeps, va, c1, g1, size1))
    pairs = [(residue(va, b1, e1, d1, size1, f, own1, own1, own1, own1)
              + residue(va, b1, e1, d1, size1, f, own1 + 1, own1 + 1, own1 + 1, own1 + 1))
             for f in range(2)]
    side = [right_mul(pairs[f], pad2[1], lambda i, j, f=f: half_of(i) + f * size2[1] == j)
            for f in range(2)]
    b2[pl.ds(me, 1)] = (left_mul(side[0] + side[1], pad2[0], coarsen) * 0.5)[None]
    all_start(b2, s_b2, r_b2, False)
    halo_start(2)
    halo_start(3)

    near_wait(b1, s_b1, r_b1, True, distances=(2, 3))
    each(own1 - 5, own1 - 2, first1_c)
    each(own1 + 4, own1 + 7, first1_c)
    each(own1 - 4, own1 - 1, functools.partial(first_sweeps, va, c1, g1, size1))
    each(own1 + 3, own1 + 6, functools.partial(first_sweeps, va, c1, g1, size1))

    all_wait(b2, s_b2, r_b2, False)

    def solve(i, source):
        e, ie, d, q, g, c, u, w = coarse[i]
        size, pad, n = sizes[2 + i], pads[2 + i], counts[i]

        def begin(p):
            value = q[p] * source[p]
            c[p] = value
            u[p + 1] = value

        each(0, n, begin, 8)

        def full(src, dst):
            def one(p):
                now = src[p]
                total = src[p - 1] + src[p + 1] + nsum(now, size, 2)
                dst[p] = (1.0 - OMEGA) * now + c[p - 1] + g[p - 1] * total

            each(1, n + 1, one, 8)

        if i == 2:
            now, then = u, w
            for _ in range(COARSE_SWEEPS - 1):
                full(now, then)
                now, then = then, now
            return now
        full(u, w)
        below = (b3, b4)[i]

        def rest_of(p):
            now = w[p + 1]
            total = w[p] + w[p + 2] + nsum(now, size, 2)
            return source[p] + e[p + 1] * total - d[p] * now

        def down(p):
            below[p] = restrict2(rest_of(2 * p) + rest_of(2 * p + 1), pads[3 + i]) * 0.5

        each(0, counts[i + 1], down, 4)
        fix = solve(i + 1, below)
        fix_inv = coarse[i + 1][1]

        def up(p):
            add = prolong2(fix[p + 1] * fix_inv[p], pad)
            w[2 * p + 1] = w[2 * p + 1] + e[2 * p + 1] * add
            w[2 * p + 2] = w[2 * p + 2] + e[2 * p + 2] * add

        each(0, counts[i + 1], up, 4)
        full(w, u)
        full(u, w)
        return w

    top = solve(0, b2)
    top_inv = coarse[0][1]
    halo_pass(2)
    halo_pass(3)

    def correct1(k):
        at = jnp.clip(me - 2 + k, 0, ns - 1)
        p = own1 - 4 + 2 * k
        rows = left_mul(top[at + 1] * top_inv[at], pad1[0], refine)
        for f in range(2):
            add = right_mul(rows, pad1[1], lambda i, j, f=f: i == f * size2[1] + half_of(j))
            va[f, p] = va[f, p] + e1[p] * add
            va[f, p + 1] = va[f, p + 1] + e1[p + 1] * add

    each(0, 5, correct1)
    each(own1 - 3, own1 + 5, functools.partial(sweep, va, c1, g1, vb, size1))
    each(own1 - 2, own1 + 4, functools.partial(sweep, vb, c1, g1, va, size1))

    halo_wait(2)
    halo_wait(3)
    each(0, half, first0_c)
    each(2 * cx + half, 3 * cx, first0_c)
    each(1, cx - 1, functools.partial(first_sweeps, ua, c0, g0, size0))
    each(2 * cx + 1, 3 * cx - 1, functools.partial(first_sweeps, ua, c0, g0, size0))

    def correct0(f, l, planes):
        add = prolong2(va[f, l] * ie1[l], size0)
        for p in planes:
            ua[f, p] = ua[f, p] + e0[p + 1] * add

    for f in range(2):
        correct0(f, own1 - 2, (1,))
        correct0(f, own1 + 3, (3 * cx - 2,))

    def middle(k):
        p = 2 + 2 * k
        both(lambda f: correct0(f, own1 - 1 + k, (p, p + 1)))

    each(0, 4, middle)
    each(2, 3 * cx - 2, functools.partial(sweep, ua, c0, g0, ub, size0))
    each(3, 3 * cx - 3, functools.partial(sweep, ub, c0, g0, ua, size0))

    def heads(p):
        inv = ie0[p + 1]
        ub[0, p] = ua[0, p] * inv
        ub[1, p] = ua[1, p] * inv

    each(cx - 1, 2 * cx + 1, heads)

    iy, iz = iota(size0, 0), iota(size0, 1)
    y_end = (iy == 0) | (iy == size0[0] - 1)

    def gradient(p, carry):
        plain, by_y, by_z = carry
        h, a, e = ub[0, p], ub[1, p], e0[p + 1]
        head_ref[0, p - cx] = h
        adj_ref[0, p - cx] = a
        lower = e * e0[p] * (h - ub[0, p - 1]) * (a - ub[1, p - 1])
        upper = e * e0[p + 2] * (h - ub[0, p + 1]) * (a - ub[1, p + 1])
        x_now = first0 + p
        edge = 2.0 * ua[0, p] * ua[1, p]
        ends = jnp.where(x_now == 0, 1.0, 0.0) + jnp.where(x_now == last0, 1.0, 0.0)
        plain = plain + 0.5 * (lower + upper) + edge * (ends + jnp.where(y_end, 1.0, 0.0))
        by_y = by_y + e * roll(e, 1, 0) * (h - roll(h, 1, 0)) * (a - roll(a, 1, 0))
        by_z = by_z + e * roll(e, 1, 1) * (h - roll(h, 1, 1)) * (a - roll(a, 1, 1))
        return plain, by_y, by_z

    plain, by_y, by_z = lax.fori_loop(cx, 2 * cx, gradient, (zero0, zero0, zero0))
    by_y = jnp.where(iy > 0, by_y, 0.0)
    by_z = jnp.where(iz > 0, by_z, 0.0)
    cells = plain + 0.5 * (by_y + roll(by_y, -1, 0) + by_z + roll(by_z, -1, 1))
    zy, zz = zone_ref.shape[1:]
    quarter = lambda i, j: jnp.right_shift(i, 2) == j
    zone = right_mul(left_mul(cells, zy, quarter, 3), zz, quarter, 3)
    weight_sum = weight_ref[0]
    for w in range(1, weight_ref.shape[0]):
        weight_sum = weight_sum + weight_ref[w]
    own = jnp.full(zone.shape, weight_ref[node], jnp.int32).astype(F32)
    portion = own / jnp.full(zone.shape, weight_sum, jnp.int32).astype(F32)
    own_zone[...] = -(portion * zone)
    zone_copy = pltpu.make_async_remote_copy(
        src_ref=own_zone, dst_ref=other_zone, send_sem=s_z, recv_sem=r_z,
        device_id={"node": 1 - node}, device_id_type=pl.DeviceIdType.MESH)
    zone_copy.start()

    for i in range(4):
        halo_sent(i)

    near_sent(l1, s_l1, r_l1, False)
    near_sent(b1, s_b1, r_b1, True)
    all_sent(l2, s_l2, r_l2, False)
    all_sent(b2, s_b2, r_b2, False)
    zone_copy.wait()
    zone_ref[0] = own_zone[...] + other_zone[...]


def body(ns, field_seeds, quad_weight, recharge, well_cells, well_rates, sensitivity):
    cx, ny, nz = recharge.shape
    sizes = [(ny >> l, nz >> l) for l in range(LEVELS)]
    pads = [(max(y, 8), max(z, 128)) for y, z in sizes]
    wide = 3 * cx
    near = 4 * REACH + 2
    vmem, smem = pltpu.VMEM, pltpu.SMEM
    p0, p1, p2 = pads[:3]
    dma = pltpu.SemaphoreType.DMA
    scratch = [
        vmem((2, wide) + p0, F32), vmem((wide + 2,) + p0, F32), vmem((wide,) + p0, F32),
        vmem((wide,) + p0, F32), vmem((wide,) + p0, F32), vmem((2, wide) + p0, F32),
        vmem((2, wide) + p0, F32), vmem((2, wide) + p0, F32), vmem((wide + 2,) + p0, F32),
        vmem((wide + 2,) + p0, F32), vmem((ns // 2,) + pads[3], F32),
        vmem((2, near) + p1, F32), vmem((near,) + p1, F32), vmem((near,) + p1, F32),
        vmem((near,) + p1, F32), vmem((near,) + p1, F32), vmem((near,) + p1, F32),
        vmem((near,) + p1, F32), vmem((2, near) + p1, F32), vmem((2, near) + p1, F32),
        vmem((2, near) + p1, F32), vmem((ns // 4,) + pads[4], F32),
        vmem((ns,) + p2, F32), vmem((ns,) + p2, F32),
    ]
    for i in range(3):
        n, pad = ns >> i, pads[2 + i]
        scratch += [vmem((n + 2,) + pad, F32), vmem((n,) + pad, F32), vmem((n,) + pad, F32),
                    vmem((n,) + pad, F32), vmem((n,) + pad, F32), vmem((n,) + pad, F32),
                    vmem((n + 2,) + pad, F32), vmem((n + 2,) + pad, F32)]
    zone = (ny // 4, nz // 4)
    scratch += [vmem(zone, F32), vmem(zone, F32)]
    spread = 2 * REACH + 1
    scratch += [dma((8,)), dma((8,)), dma((2,)), dma((spread,)), dma((spread,)), dma((spread,)), dma((spread,)),
                dma((ns,)), dma((ns,)), dma((ns,)), dma((ns,)), dma, dma]
    in_v, in_s = pl.BlockSpec(memory_space=vmem), pl.BlockSpec(memory_space=smem)
    field = jax.ShapeDtypeStruct((1, cx, ny, nz), F32)
    return pl.pallas_call(
        functools.partial(kernel, ns, sizes, pads),
        out_shape=(field, field, jax.ShapeDtypeStruct((1,) + zone, F32)),
        in_specs=[in_s, in_s, pl.BlockSpec(memory_space=pl.ANY), in_s, in_s,
                  pl.BlockSpec(memory_space=pl.ANY)],
        out_specs=(in_v, in_v, in_v),
        scratch_shapes=scratch,
        compiler_params=pltpu.CompilerParams(
            collective_id=0, has_side_effects=True, vmem_limit_bytes=48 * 1024 * 1024),
    )(field_seeds, quad_weight, recharge, well_cells, well_rates, sensitivity)


def solution(mesh):
    placed = (
        P(("groups", "node")),
        P("groups"),
        P(("groups", "slab"), None, None),
        P(("groups", "slab")),
        P(("groups", "slab")),
        P(("groups", "slab"), None, None),
    )
    return jax.shard_map(
        functools.partial(body, mesh.shape["slab"]),
        mesh=mesh,
        in_specs=placed,
        out_specs=(
            P(("groups", "node"), "slab", None, None),
            P(("groups", "node"), "slab", None, None),
            P(("groups", "slab"), None, None),
        ),
        check_vma=False,
    )
```

```python
import functools

import jax
import jax.numpy as jnp
from jax import lax
from jax.experimental import pallas as pl
from jax.experimental.pallas import tpu as pltpu
from jax.sharding import PartitionSpec as P

LEVELS = 5
SWEEPS = 2
COARSE_SWEEPS = 8
OMEGA = 0.8
REACH = 3

F32 = jnp.float32


def iota(shape, axis):
    return lax.broadcasted_iota(jnp.int32, shape, axis)


def matrix(rows, cols, rule, dtype=jnp.bfloat16):
    shape = (rows, cols)
    return jnp.where(rule(iota(shape, 0), iota(shape, 1)), 1.0, 0.0).astype(dtype)


def half_of(i):
    return jnp.right_shift(i, 1)


def coarsen(i, j):
    return half_of(i) == j


def refine(i, j):
    return i == half_of(j)


def split(x, terms):
    parts = []
    for _ in range(terms):
        part = x.astype(jnp.bfloat16)
        parts.append(part)
        x = x - part.astype(F32)
    return parts


def right_mul(x, cols, rule, terms=2):
    m = matrix(x.shape[1], cols, rule)
    out = None
    for part in split(x, terms):
        y = jnp.dot(part, m, preferred_element_type=F32)
        out = y if out is None else out + y
    return out


def left_mul(x, rows, rule, terms=2):
    m = matrix(rows, x.shape[0], lambda i, j: rule(j, i))
    out = None
    for part in split(x, terms):
        y = jnp.dot(m, part, preferred_element_type=F32)
        out = y if out is None else out + y
    return out


def restrict2(x, shape, terms=2):
    return left_mul(right_mul(x, shape[1], coarsen, terms), shape[0], coarsen, terms)


def prolong2(x, shape, terms=2):
    return right_mul(left_mul(x, shape[0], refine, terms), shape[1], refine, terms)


def roll(x, shift, axis):
    return pltpu.roll(x, shift % x.shape[axis], axis)


def nsum(x, size, fields=1):
    iy, iz = iota(x.shape, 0), iota(x.shape, 1)
    if fields > 1:
        iz = jnp.bitwise_and(iz, size[1] - 1)
    total = jnp.where(iy > 0, roll(x, 1, 0), 0.0)
    total = total + jnp.where(iy < size[0] - 1, roll(x, -1, 0), 0.0)
    total = total + jnp.where(iz > 0, roll(x, 1, 1), 0.0)
    return total + jnp.where(iz < size[1] - 1, roll(x, -1, 1), 0.0)


def each(start, stop, fn, unroll=2):
    def step(p, carry):
        fn(p)
        return carry

    if stop - start <= unroll:
        for p in range(start, stop):
            fn(p)
        return
    lax.fori_loop(start, stop, step, 0)


def both(fn):
    for f in range(2):
        fn(f)


def diag_plane(center, below, above, x_now, x_last, size, fields=1):
    iy = iota(center.shape, 0)
    d = below + above + nsum(center, size, fields)
    outside = jnp.where(iy == 0, 2.0, 0.0) + jnp.where(iy == size[0] - 1, 2.0, 0.0)
    ends = jnp.where(x_now == 0, 2.0, 0.0) + jnp.where(x_now == x_last, 2.0, 0.0)
    return d + (outside + ends) * center


def inside(shape, size, x_now, x_last, fields=1):
    ok = (iota(shape, 0) < size[0]) & (iota(shape, 1) < fields * size[1])
    return ok & ((x_now >= 0) & (x_now <= x_last))


def kernel(ns, sizes, pads, seed_ref, weight_ref, recharge_ref, cells_ref, rates_ref, sens_ref,
           head_ref, adj_ref, zone_ref,
           b0, e0, d0, q0, g0, c0, ua, ub, ie0, b3,
           b1, l1, e1, ie1, d1, q1, g1, c1, va, vb, b4,
           l2, b2, *rest):
    coarse = [rest[8 * i: 8 * i + 8] for i in range(3)]
    own_zone, other_zone = rest[24:26]
    s_halo, r_halo, s_in, s_b1, r_b1, s_l2, r_l2, s_b2, r_b2, s_z, r_z = rest[26:]
    me = lax.axis_index("slab")
    node = lax.axis_index("node")
    size0, size1, size2 = sizes[:3]
    pad1, pad2 = pads[1], pads[2]
    cx = recharge_ref.shape[0]
    last0 = cx * ns - 1
    own1 = 2 * REACH
    last1 = 2 * ns - 1

    def remote(src, dst, send, recv, slab):
        return pltpu.make_async_remote_copy(
            src_ref=src, dst_ref=dst, send_sem=send, recv_sem=recv,
            device_id={"slab": slab}, device_id_type=pl.DeviceIdType.MESH)

    zero0 = jnp.zeros(size0, F32)
    zero1 = jnp.zeros(pad1, F32)

    @pl.when(me == 0)
    def _():
        each(0, cx, lambda p: both(lambda f: b0.__setitem__((f, p), zero0)))

    @pl.when(me == ns - 1)
    def _():
        each(2 * cx, 3 * cx, lambda p: both(lambda f: b0.__setitem__((f, p), zero0)))

    def clear1(p):
        b1[0, p] = zero1
        b1[1, p] = zero1

    each(0, 2 * own1 + 2, clear1)

    barrier = pltpu.get_barrier_semaphore()

    def greet(k):
        peer = lax.rem(me + k, ns)
        pl.semaphore_signal(barrier, inc=1, device_id={"slab": peer},
                            device_id_type=pl.DeviceIdType.MESH)

    each(1, ns, greet)
    pl.semaphore_signal(barrier, inc=1, device_id={"node": 1 - node},
                        device_id_type=pl.DeviceIdType.MESH)

    loads = [pltpu.make_async_copy(ref, b0.at[f, pl.ds(cx, cx)], s_in.at[f])
             for f, ref in enumerate((recharge_ref, sens_ref))]
    for load in loads:
        load.start()

    place = iota(size0, 0) * size0[1] + iota(size0, 1)

    def sources(p):
        value = b0[0, cx + p]
        here = place + p * (size0[0] * size0[1])
        for w in range(cells_ref.shape[0]):
            value = value + jnp.where(here == cells_ref[w], rates_ref[w], 0.0)
        b0[0, cx + p] = value

    for load in loads:
        load.wait()
    each(0, cx, sources)
    pl.semaphore_wait(barrier, ns)

    half = cx // 2
    halo = [(1, cx + half, half, 0), (-1, cx, 2 * cx, 1),
            (1, cx, 0, 2), (-1, cx + half, 2 * cx + half, 3)]

    def halo_copy(way, src, dst, i, slab):
        field = pl.ds(node, 1)
        return remote(b0.at[field, pl.ds(src, half)], b0.at[field, pl.ds(dst, half)],
                      s_halo.at[i], r_halo.at[i], slab)

    def pass_copy(way, src, dst, i, slab, field):
        at = b0.at[pl.ds(field, 1), pl.ds(dst, half)]
        return pltpu.make_async_remote_copy(
            src_ref=at, dst_ref=at, send_sem=s_halo.at[4 + i], recv_sem=r_halo.at[4 + i],
            device_id={"node": 1 - node}, device_id_type=pl.DeviceIdType.MESH)

    def in_range(slab):
        return (slab >= 0) & (slab < ns)

    def halo_start(i):
        way = halo[i][0]

        @pl.when(in_range(me + way))
        def _():
            halo_copy(*halo[i], me + way).start()

    def halo_pass(i):
        way = halo[i][0]

        @pl.when(in_range(me - way))
        def _():
            halo_copy(*halo[i], me - way).wait_recv()
            pass_copy(*halo[i], me, node).start()

    def halo_wait(i):
        way = halo[i][0]

        @pl.when(in_range(me - way))
        def _():
            pass_copy(*halo[i], me, 1 - node).wait_recv()

    def halo_sent(i):
        way = halo[i][0]

        @pl.when(in_range(me + way))
        def _():
            halo_copy(*halo[i], me + way).wait_send()

        @pl.when(in_range(me - way))
        def _():
            pass_copy(*halo[i], me, node).wait_send()

    for i in range(2):
        halo_start(i)

    def near_copy(ref, send, recv, lead, d, slab):
        src, dst = pl.ds(own1, 2), pl.ds(own1 - 2 * d, 2)
        index = (slice(None),) if lead else ()
        return remote(ref.at[index + (src,)], ref.at[index + (dst,)],
                      send.at[d + REACH], recv.at[d + REACH], slab)

    steps = [s * d for d in range(1, REACH + 1) for s in (1, -1)]

    def near_start(*args):
        for d in steps:
            @pl.when(in_range(me + d))
            def _():
                near_copy(*args, d, me + d).start()

    def near_wait(*args, distances):
        for d in steps:
            if abs(d) in distances:
                @pl.when(in_range(me - d))
                def _():
                    near_copy(*args, d, me - d).wait_recv()

    def near_sent(*args):
        for d in steps:
            @pl.when(in_range(me + d))
            def _():
                near_copy(*args, d, me + d).wait_send()

    def all_copy(ref, send, recv, lead, k, slab, owner):
        index = (slice(None),) if lead else ()
        at = ref.at[index + (pl.ds(owner, 1),)]
        return remote(at, at, send.at[k], recv.at[k], slab)

    def all_start(*args):
        each(1, ns, lambda k: all_copy(*args, k, lax.rem(me + k, ns), me).start())

    def all_wait(*args):
        def wait(k):
            peer = lax.rem(me - k + ns, ns)
            all_copy(*args, k, peer, peer).wait_recv()

        each(1, ns, wait)

    def all_sent(*args):
        each(1, ns, lambda k: all_copy(*args, k, lax.rem(me + k, ns), me).wait_send())

    seed_part = seed_ref[0] * 277803737 + 1013904223
    hashed_place = place * 747796405
    first0 = me * cx - cx

    def logk_at(x_now):
        q = hashed_place + (x_now * (size0[0] * size0[1]) * 747796405 + seed_part)
        q = jnp.bitwise_xor(q, lax.shift_right_logical(q, jnp.full(size0, 15, jnp.int32)))
        q = q * 1274126177
        q = jnp.bitwise_xor(q, lax.shift_right_logical(q, jnp.full(size0, 13, jnp.int32)))
        low = jnp.bitwise_and(q, 65535)
        return 3.0 * (low.astype(F32) / 65536.0) - 1.5

    def logk_plane(p):
        x_now = first0 - 1 + p
        logk = logk_at(x_now)
        known = (x_now >= 0) & (x_now <= last0)
        e0[p] = jnp.where(known, jnp.exp(0.5 * logk), 0.0)
        ie0[p] = jnp.exp(-0.5 * logk)

    each(0, 3 * cx + 2, logk_plane)
    first1 = 2 * me - own1

    def logk1_plane(p):
        x_now = 2 * (first1 + p)
        l1[p] = restrict2(logk_at(x_now) + logk_at(x_now + 1), pad1, 3) * 0.125

    each(own1, own1 + 2, logk1_plane)
    both_fields = right_mul(l1[own1] + l1[own1 + 1], pad2[1],
                            lambda i, j: half_of(i) == jnp.bitwise_and(j, size2[1] - 1), 3)
    l2[pl.ds(me, 1)] = (left_mul(both_fields, pad2[0], coarsen, 3) * 0.125)[None]
    all_start(l2, s_l2, r_l2, False)

    def operator0(p):
        x_now = first0 + p
        center = e0[p + 1]
        d = diag_plane(center, e0[p], e0[p + 2], x_now, last0, size0)
        known = (x_now >= 0) & (x_now <= last0)
        q = jnp.where(known, OMEGA / d, 0.0)
        d0[p] = d
        q0[p] = q
        g0[p] = q * center

    each(0, 3 * cx, operator0)

    def first0_c(p):
        q = q0[p]
        c0[0, p] = q * b0[0, p]
        c0[1, p] = q * b0[1, p]

    def first_sweeps(u, c, g, size, p):
        gain = g[p]

        def one(f):
            now = c[f, p]
            total = c[f, p - 1] + c[f, p + 1] + nsum(now, size)
            u[f, p] = (2.0 - OMEGA) * now + gain * total

        both(one)

    def sweep(u, c, g, out, size, p, gp=None, cp=None):
        gp = p if gp is None else gp
        cp = p if cp is None else cp
        gain = g[gp]

        def one(f):
            now = u[f, p]
            total = u[f, p - 1] + u[f, p + 1] + nsum(now, size)
            out[f, p] = (1.0 - OMEGA) * now + c[f, cp] + gain * total

        both(one)

    def residue(u, b, e, d, size, f, p, ep, dp, bp):
        now = u[f, p]
        total = u[f, p - 1] + u[f, p + 1] + nsum(now, size)
        return b[f, bp] + e[ep] * total - d[dp] * now

    each(cx, 2 * cx, first0_c)

    each(0, own1, logk1_plane)
    halo_pass(0)
    halo_pass(1)
    each(own1 + 2, 2 * own1 + 2, logk1_plane)
    each(cx + 1, 2 * cx - 1, functools.partial(first_sweeps, ua, c0, g0, size0))
    halo_wait(0)
    halo_wait(1)
    each(half, cx, first0_c)
    each(2 * cx, 2 * cx + half, first0_c)
    each(cx - 1, cx + 1, functools.partial(first_sweeps, ua, c0, g0, size0))
    each(2 * cx - 1, 2 * cx + 1, functools.partial(first_sweeps, ua, c0, g0, size0))

    for f in range(2):
        for i in range(2):
            p = cx + 2 * i
            pair = (residue(ua, b0, e0, d0, size0, f, p, p + 1, p, p)
                    + residue(ua, b0, e0, d0, size0, f, p + 1, p + 2, p + 1, p + 1))
            b1[f, own1 + i] = restrict2(pair, pad1) * 0.5
    near_start(b1, s_b1, r_b1, True)

    width1 = 2 * own1 + 2

    def exp1(p):
        x_now = first1 + p
        ok = inside(pad1, size1, x_now, last1)
        logk = l1[p]
        e1[p] = jnp.where(ok, jnp.exp(0.5 * logk), 0.0)
        ie1[p] = jnp.where(ok, jnp.exp(-0.5 * logk), 0.0)

    each(0, width1, exp1)

    def operator1(p):
        x_now = first1 + p
        center = e1[p]
        d = diag_plane(center, e1[p - 1], e1[p + 1], x_now, last1, size1)
        q = jnp.where(inside(pad1, size1, x_now, last1), OMEGA / d, 0.0)
        d1[p] = d
        q1[p] = q
        g1[p] = q * center

    each(1, width1 - 1, operator1)

    all_wait(l2, s_l2, r_l2, False)
    counts = [ns >> i for i in range(3)]
    for i in range(3):
        e, ie, d, q, g, c, u, w = coarse[i]
        size, pad, n = sizes[2 + i], pads[2 + i], counts[i]
        e[0] = jnp.zeros(pad, F32)
        e[n + 1] = jnp.zeros(pad, F32)
        for ref in (u, w):
            ref[0] = jnp.zeros(pad, F32)
            ref[n + 1] = jnp.zeros(pad, F32)

        def exps(p, e=e, ie=ie, size=size, pad=pad, n=n, i=i, d=d):
            if i == 0:
                logk = l2[p]
            else:
                above = coarse[i - 1][4] if i > 1 else l2
                logk = restrict2(above[2 * p] + above[2 * p + 1], pad, 3) * 0.125
                g_now = coarse[i][4]
                g_now[p] = logk
            ok = inside(pad, size, p, n - 1, 2)
            e[p + 1] = jnp.where(ok, jnp.exp(0.5 * logk), 0.0)
            ie[p] = jnp.where(ok, jnp.exp(-0.5 * logk), 0.0)

        each(0, n, exps)
    for i in range(3):
        e, ie, d, q, g, c, u, w = coarse[i]
        size, pad, n = sizes[2 + i], pads[2 + i], counts[i]

        def ops(p, e=e, d=d, q=q, g=g, size=size, pad=pad, n=n):
            center = e[p + 1]
            dd = diag_plane(center, e[p], e[p + 2], p, n - 1, size, 2)
            qq = jnp.where(inside(pad, size, p, n - 1, 2), OMEGA / dd, 0.0)
            d[p] = dd
            q[p] = qq
            g[p] = qq * center

        each(0, n, ops)

    def first1_c(p):
        q = q1[p]
        c1[0, p] = q * b1[0, p]
        c1[1, p] = q * b1[1, p]

    near_wait(b1, s_b1, r_b1, True, distances=(1,))
    each(own1 - 2, own1 + 4, first1_c)
    each(own1 - 1, own1 + 3, functools.partial(first_sweeps, va, c1, g1, size1))
    pairs = [(residue(va, b1, e1, d1, size1, f, own1, own1, own1, own1)
              + residue(va, b1, e1, d1, size1, f, own1 + 1, own1 + 1, own1 + 1, own1 + 1))
             for f in range(2)]
    side = [right_mul(pairs[f], pad2[1], lambda i, j, f=f: half_of(i) + f * size2[1] == j)
            for f in range(2)]
    b2[pl.ds(me, 1)] = (left_mul(side[0] + side[1], pad2[0], coarsen) * 0.5)[None]
    all_start(b2, s_b2, r_b2, False)
    halo_start(2)
    halo_start(3)

    near_wait(b1, s_b1, r_b1, True, distances=(2, 3))
    each(own1 - 5, own1 - 2, first1_c)
    each(own1 + 4, own1 + 7, first1_c)
    each(own1 - 4, own1 - 1, functools.partial(first_sweeps, va, c1, g1, size1))
    each(own1 + 3, own1 + 6, functools.partial(first_sweeps, va, c1, g1, size1))

    all_wait(b2, s_b2, r_b2, False)

    def solve(i, source):
        e, ie, d, q, g, c, u, w = coarse[i]
        size, pad, n = sizes[2 + i], pads[2 + i], counts[i]

        def begin(p):
            value = q[p] * source[p]
            c[p] = value
            u[p + 1] = value

        each(0, n, begin, 8)

        def full(src, dst):
            def one(p):
                now = src[p]
                total = src[p - 1] + src[p + 1] + nsum(now, size, 2)
                dst[p] = (1.0 - OMEGA) * now + c[p - 1] + g[p - 1] * total

            each(1, n + 1, one, 8)

        if i == 2:
            now, then = u, w
            for _ in range(COARSE_SWEEPS - 1):
                full(now, then)
                now, then = then, now
            return now
        full(u, w)
        below = (b3, b4)[i]

        def rest_of(p):
            now = w[p + 1]
            total = w[p] + w[p + 2] + nsum(now, size, 2)
            return source[p] + e[p + 1] * total - d[p] * now

        def down(p):
            below[p] = restrict2(rest_of(2 * p) + rest_of(2 * p + 1), pads[3 + i]) * 0.5

        each(0, counts[i + 1], down, 4)
        fix = solve(i + 1, below)
        fix_inv = coarse[i + 1][1]

        def up(p):
            add = prolong2(fix[p + 1] * fix_inv[p], pad)
            w[2 * p + 1] = w[2 * p + 1] + e[2 * p + 1] * add
            w[2 * p + 2] = w[2 * p + 2] + e[2 * p + 2] * add

        each(0, counts[i + 1], up, 4)
        full(w, u)
        full(u, w)
        return w

    top = solve(0, b2)
    top_inv = coarse[0][1]
    halo_pass(2)
    halo_pass(3)

    def correct1(k):
        at = jnp.clip(me - 2 + k, 0, ns - 1)
        p = own1 - 4 + 2 * k
        rows = left_mul(top[at + 1] * top_inv[at], pad1[0], refine)
        for f in range(2):
            add = right_mul(rows, pad1[1], lambda i, j, f=f: i == f * size2[1] + half_of(j))
            va[f, p] = va[f, p] + e1[p] * add
            va[f, p + 1] = va[f, p + 1] + e1[p + 1] * add

    each(0, 5, correct1)
    each(own1 - 3, own1 + 5, functools.partial(sweep, va, c1, g1, vb, size1))
    each(own1 - 2, own1 + 4, functools.partial(sweep, vb, c1, g1, va, size1))

    halo_wait(2)
    halo_wait(3)
    each(0, half, first0_c)
    each(2 * cx + half, 3 * cx, first0_c)
    each(1, cx - 1, functools.partial(first_sweeps, ua, c0, g0, size0))
    each(2 * cx + 1, 3 * cx - 1, functools.partial(first_sweeps, ua, c0, g0, size0))

    def correct0(f, l, planes):
        add = prolong2(va[f, l] * ie1[l], size0)
        for p in planes:
            ua[f, p] = ua[f, p] + e0[p + 1] * add

    for f in range(2):
        correct0(f, own1 - 2, (1,))
        correct0(f, own1 + 3, (3 * cx - 2,))

    def middle(k):
        p = 2 + 2 * k
        both(lambda f: correct0(f, own1 - 1 + k, (p, p + 1)))

    each(0, 4, middle)
    each(2, 3 * cx - 2, functools.partial(sweep, ua, c0, g0, ub, size0))
    each(3, 3 * cx - 3, functools.partial(sweep, ub, c0, g0, ua, size0))

    def heads(p):
        inv = ie0[p + 1]
        ub[0, p] = ua[0, p] * inv
        ub[1, p] = ua[1, p] * inv

    each(cx - 1, 2 * cx + 1, heads)

    iy, iz = iota(size0, 0), iota(size0, 1)
    y_end = (iy == 0) | (iy == size0[0] - 1)

    def gradient(p, carry):
        plain, by_y, by_z = carry
        h, a, e = ub[0, p], ub[1, p], e0[p + 1]
        head_ref[0, p - cx] = h
        adj_ref[0, p - cx] = a
        lower = e * e0[p] * (h - ub[0, p - 1]) * (a - ub[1, p - 1])
        upper = e * e0[p + 2] * (h - ub[0, p + 1]) * (a - ub[1, p + 1])
        x_now = first0 + p
        edge = 2.0 * ua[0, p] * ua[1, p]
        ends = jnp.where(x_now == 0, 1.0, 0.0) + jnp.where(x_now == last0, 1.0, 0.0)
        plain = plain + 0.5 * (lower + upper) + edge * (ends + jnp.where(y_end, 1.0, 0.0))
        by_y = by_y + e * roll(e, 1, 0) * (h - roll(h, 1, 0)) * (a - roll(a, 1, 0))
        by_z = by_z + e * roll(e, 1, 1) * (h - roll(h, 1, 1)) * (a - roll(a, 1, 1))
        return plain, by_y, by_z

    plain, by_y, by_z = lax.fori_loop(cx, 2 * cx, gradient, (zero0, zero0, zero0))
    by_y = jnp.where(iy > 0, by_y, 0.0)
    by_z = jnp.where(iz > 0, by_z, 0.0)
    cells = plain + 0.5 * (by_y + roll(by_y, -1, 0) + by_z + roll(by_z, -1, 1))
    zy, zz = zone_ref.shape[1:]
    quarter = lambda i, j: jnp.right_shift(i, 2) == j
    zone = right_mul(left_mul(cells, zy, quarter, 3), zz, quarter, 3)
    weight_sum = weight_ref[0]
    for w in range(1, weight_ref.shape[0]):
        weight_sum = weight_sum + weight_ref[w]
    own = jnp.full(zone.shape, weight_ref[node], jnp.int32).astype(F32)
    portion = own / jnp.full(zone.shape, weight_sum, jnp.int32).astype(F32)
    own_zone[...] = -(portion * zone)
    zone_copy = pltpu.make_async_remote_copy(
        src_ref=own_zone, dst_ref=other_zone, send_sem=s_z, recv_sem=r_z,
        device_id={"node": 1 - node}, device_id_type=pl.DeviceIdType.MESH)
    zone_copy.start()

    for i in range(4):
        halo_sent(i)

    near_sent(b1, s_b1, r_b1, True)
    all_sent(l2, s_l2, r_l2, False)
    all_sent(b2, s_b2, r_b2, False)
    zone_copy.wait()
    zone_ref[0] = own_zone[...] + other_zone[...]


def body(ns, field_seeds, quad_weight, recharge, well_cells, well_rates, sensitivity):
    cx, ny, nz = recharge.shape
    sizes = [(ny >> l, nz >> l) for l in range(LEVELS)]
    pads = [(max(y, 8), max(z, 128)) for y, z in sizes]
    wide = 3 * cx
    near = 4 * REACH + 2
    vmem, smem = pltpu.VMEM, pltpu.SMEM
    p0, p1, p2 = pads[:3]
    dma = pltpu.SemaphoreType.DMA
    scratch = [
        vmem((2, wide) + p0, F32), vmem((wide + 2,) + p0, F32), vmem((wide,) + p0, F32),
        vmem((wide,) + p0, F32), vmem((wide,) + p0, F32), vmem((2, wide) + p0, F32),
        vmem((2, wide) + p0, F32), vmem((2, wide) + p0, F32),
        vmem((wide + 2,) + p0, F32), vmem((ns // 2,) + pads[3], F32),
        vmem((2, near) + p1, F32), vmem((near,) + p1, F32), vmem((near,) + p1, F32),
        vmem((near,) + p1, F32), vmem((near,) + p1, F32), vmem((near,) + p1, F32),
        vmem((near,) + p1, F32), vmem((2, near) + p1, F32), vmem((2, near) + p1, F32),
        vmem((2, near) + p1, F32), vmem((ns // 4,) + pads[4], F32),
        vmem((ns,) + p2, F32), vmem((ns,) + p2, F32),
    ]
    for i in range(3):
        n, pad = ns >> i, pads[2 + i]
        scratch += [vmem((n + 2,) + pad, F32), vmem((n,) + pad, F32), vmem((n,) + pad, F32),
                    vmem((n,) + pad, F32), vmem((n,) + pad, F32), vmem((n,) + pad, F32),
                    vmem((n + 2,) + pad, F32), vmem((n + 2,) + pad, F32)]
    zone = (ny // 4, nz // 4)
    scratch += [vmem(zone, F32), vmem(zone, F32)]
    spread = 2 * REACH + 1
    scratch += [dma((8,)), dma((8,)), dma((2,)), dma((spread,)), dma((spread,)),
                dma((ns,)), dma((ns,)), dma((ns,)), dma((ns,)), dma, dma]
    in_v, in_s = pl.BlockSpec(memory_space=vmem), pl.BlockSpec(memory_space=smem)
    field = jax.ShapeDtypeStruct((1, cx, ny, nz), F32)
    return pl.pallas_call(
        functools.partial(kernel, ns, sizes, pads),
        out_shape=(field, field, jax.ShapeDtypeStruct((1,) + zone, F32)),
        in_specs=[in_s, in_s, pl.BlockSpec(memory_space=pl.ANY), in_s, in_s,
                  pl.BlockSpec(memory_space=pl.ANY)],
        out_specs=(in_v, in_v, in_v),
        scratch_shapes=scratch,
        compiler_params=pltpu.CompilerParams(
            collective_id=0, has_side_effects=True, vmem_limit_bytes=48 * 1024 * 1024),
    )(field_seeds, quad_weight, recharge, well_cells, well_rates, sensitivity)


def solution(mesh):
    placed = (
        P(("groups", "node")),
        P("groups"),
        P(("groups", "slab"), None, None),
        P(("groups", "slab")),
        P(("groups", "slab")),
        P(("groups", "slab"), None, None),
    )
    return jax.shard_map(
        functools.partial(body, mesh.shape["slab"]),
        mesh=mesh,
        in_specs=placed,
        out_specs=(
            P(("groups", "node"), "slab", None, None),
            P(("groups", "node"), "slab", None, None),
            P(("groups", "slab"), None, None),
        ),
        check_vma=False,
    )
```

```python
import functools

import jax
import jax.numpy as jnp
from jax import lax
from jax.experimental import pallas as pl
from jax.experimental.pallas import tpu as pltpu
from jax.sharding import PartitionSpec as P

LEVELS = 5
SWEEPS = 2
COARSE_SWEEPS = 8
OMEGA = 0.8
REACH = 3

F32 = jnp.float32


def iota(shape, axis):
    return lax.broadcasted_iota(jnp.int32, shape, axis)


def matrix(rows, cols, rule, dtype=jnp.bfloat16):
    shape = (rows, cols)
    return jnp.where(rule(iota(shape, 0), iota(shape, 1)), 1.0, 0.0).astype(dtype)


KEPT = {}


def half_of(i):
    return jnp.right_shift(i, 1)


def coarsen(i, j):
    return half_of(i) == j


def refine(i, j):
    return i == half_of(j)


def split(x, terms):
    parts = []
    for _ in range(terms):
        part = x.astype(jnp.bfloat16)
        parts.append(part)
        x = x - part.astype(F32)
    return parts


def right_mul(x, cols, rule, terms=2):
    m = KEPT.get((x.shape[1], cols, rule))
    m = matrix(x.shape[1], cols, rule) if m is None else m
    out = None
    for part in split(x, terms):
        y = jnp.dot(part, m, preferred_element_type=F32)
        out = y if out is None else out + y
    return out


def left_mul(x, rows, rule, terms=2):
    m = KEPT.get((rule, rows, x.shape[0]))
    m = matrix(rows, x.shape[0], lambda i, j: rule(j, i)) if m is None else m
    out = None
    for part in split(x, terms):
        y = jnp.dot(m, part, preferred_element_type=F32)
        out = y if out is None else out + y
    return out


def restrict2(x, shape, terms=2):
    return left_mul(right_mul(x, shape[1], coarsen, terms), shape[0], coarsen, terms)


def prolong2(x, shape, terms=2):
    return right_mul(left_mul(x, shape[0], refine, terms), shape[1], refine, terms)


def roll(x, shift, axis):
    return pltpu.roll(x, shift % x.shape[axis], axis)


def nsum(x, size, fields=1):
    iy, iz = iota(x.shape, 0), iota(x.shape, 1)
    if fields > 1:
        iz = jnp.bitwise_and(iz, size[1] - 1)
    total = jnp.where(iy > 0, roll(x, 1, 0), 0.0)
    total = total + jnp.where(iy < size[0] - 1, roll(x, -1, 0), 0.0)
    total = total + jnp.where(iz > 0, roll(x, 1, 1), 0.0)
    return total + jnp.where(iz < size[1] - 1, roll(x, -1, 1), 0.0)


def each(start, stop, fn, unroll=2):
    def step(p, carry):
        fn(p)
        return carry

    if stop - start <= unroll:
        for p in range(start, stop):
            fn(p)
        return
    lax.fori_loop(start, stop, step, 0)


def both(fn):
    for f in range(2):
        fn(f)


def diag_plane(center, below, above, x_now, x_last, size, fields=1):
    iy = iota(center.shape, 0)
    d = below + above + nsum(center, size, fields)
    outside = jnp.where(iy == 0, 2.0, 0.0) + jnp.where(iy == size[0] - 1, 2.0, 0.0)
    ends = jnp.where(x_now == 0, 2.0, 0.0) + jnp.where(x_now == x_last, 2.0, 0.0)
    return d + (outside + ends) * center


def inside(shape, size, x_now, x_last, fields=1):
    ok = (iota(shape, 0) < size[0]) & (iota(shape, 1) < fields * size[1])
    return ok & ((x_now >= 0) & (x_now <= x_last))


def kernel(ns, sizes, pads, seed_ref, weight_ref, recharge_ref, cells_ref, rates_ref, sens_ref,
           head_ref, adj_ref, zone_ref,
           b0, e0, d0, q0, g0, c0, ua, ub, ie0, b3,
           b1, l1, e1, ie1, d1, q1, g1, c1, va, vb, b4,
           l2, b2, *rest):
    coarse = [rest[8 * i: 8 * i + 8] for i in range(3)]
    own_zone, other_zone = rest[24:26]
    s_halo, r_halo, s_in, s_b1, r_b1, s_l2, r_l2, s_b2, r_b2, s_z, r_z = rest[26:]
    me = lax.axis_index("slab")
    node = lax.axis_index("node")
    size0, size1, size2 = sizes[:3]
    pad1, pad2 = pads[1], pads[2]
    cx = recharge_ref.shape[0]
    last0 = cx * ns - 1
    own1 = 2 * REACH
    last1 = 2 * ns - 1

    def remote(src, dst, send, recv, slab):
        return pltpu.make_async_remote_copy(
            src_ref=src, dst_ref=dst, send_sem=send, recv_sem=recv,
            device_id={"slab": slab}, device_id_type=pl.DeviceIdType.MESH)

    KEPT.clear()
    built = {}
    for rule, fine, other in ((coarsen, 0, 1), (refine, 1, 0)):
        (y, z), (rows, cols) = pads[fine], pads[other]
        built[(z, cols, rule)] = matrix(z, cols, rule)
        built[(rule, rows, y)] = matrix(rows, y, lambda i, j, rule=rule: rule(j, i))
    KEPT.update(built)

    zero0 = jnp.zeros(size0, F32)
    zero1 = jnp.zeros(pad1, F32)

    @pl.when(me == 0)
    def _():
        each(0, cx, lambda p: both(lambda f: b0.__setitem__((f, p), zero0)))

    @pl.when(me == ns - 1)
    def _():
        each(2 * cx, 3 * cx, lambda p: both(lambda f: b0.__setitem__((f, p), zero0)))

    def clear1(p):
        b1[0, p] = zero1
        b1[1, p] = zero1

    each(0, 2 * own1 + 2, clear1)

    barrier = pltpu.get_barrier_semaphore()

    def greet(k):
        peer = lax.rem(me + k, ns)
        pl.semaphore_signal(barrier, inc=1, device_id={"slab": peer},
                            device_id_type=pl.DeviceIdType.MESH)

    each(1, ns, greet)
    pl.semaphore_signal(barrier, inc=1, device_id={"node": 1 - node},
                        device_id_type=pl.DeviceIdType.MESH)

    loads = [pltpu.make_async_copy(ref, b0.at[f, pl.ds(cx, cx)], s_in.at[f])
             for f, ref in enumerate((recharge_ref, sens_ref))]
    for load in loads:
        load.start()

    place = iota(size0, 0) * size0[1] + iota(size0, 1)

    def sources(p):
        value = b0[0, cx + p]
        here = place + p * (size0[0] * size0[1])
        for w in range(cells_ref.shape[0]):
            value = value + jnp.where(here == cells_ref[w], rates_ref[w], 0.0)
        b0[0, cx + p] = value

    for load in loads:
        load.wait()
    each(0, cx, sources)
    pl.semaphore_wait(barrier, ns)

    half = cx // 2
    halo = [(1, cx + half, half, 0), (-1, cx, 2 * cx, 1),
            (1, cx, 0, 2), (-1, cx + half, 2 * cx + half, 3)]

    def halo_copy(way, src, dst, i, slab):
        field = pl.ds(node, 1)
        return remote(b0.at[field, pl.ds(src, half)], b0.at[field, pl.ds(dst, half)],
                      s_halo.at[i], r_halo.at[i], slab)

    def pass_copy(way, src, dst, i, slab, field):
        at = b0.at[pl.ds(field, 1), pl.ds(dst, half)]
        return pltpu.make_async_remote_copy(
            src_ref=at, dst_ref=at, send_sem=s_halo.at[4 + i], recv_sem=r_halo.at[4 + i],
            device_id={"node": 1 - node}, device_id_type=pl.DeviceIdType.MESH)

    def in_range(slab):
        return (slab >= 0) & (slab < ns)

    def halo_start(i):
        way = halo[i][0]

        @pl.when(in_range(me + way))
        def _():
            halo_copy(*halo[i], me + way).start()

    def halo_pass(i):
        way = halo[i][0]

        @pl.when(in_range(me - way))
        def _():
            halo_copy(*halo[i], me - way).wait_recv()
            pass_copy(*halo[i], me, node).start()

    def halo_wait(i):
        way = halo[i][0]

        @pl.when(in_range(me - way))
        def _():
            pass_copy(*halo[i], me, 1 - node).wait_recv()

    def halo_sent(i):
        way = halo[i][0]

        @pl.when(in_range(me + way))
        def _():
            halo_copy(*halo[i], me + way).wait_send()

        @pl.when(in_range(me - way))
        def _():
            pass_copy(*halo[i], me, node).wait_send()

    for i in range(2):
        halo_start(i)

    def near_copy(ref, send, recv, lead, d, slab):
        src, dst = pl.ds(own1, 2), pl.ds(own1 - 2 * d, 2)
        index = (slice(None),) if lead else ()
        return remote(ref.at[index + (src,)], ref.at[index + (dst,)],
                      send.at[d + REACH], recv.at[d + REACH], slab)

    steps = [s * d for d in range(1, REACH + 1) for s in (1, -1)]

    def near_start(*args):
        for d in steps:
            @pl.when(in_range(me + d))
            def _():
                near_copy(*args, d, me + d).start()

    def near_wait(*args, distances):
        for d in steps:
            if abs(d) in distances:
                @pl.when(in_range(me - d))
                def _():
                    near_copy(*args, d, me - d).wait_recv()

    def near_sent(*args):
        for d in steps:
            @pl.when(in_range(me + d))
            def _():
                near_copy(*args, d, me + d).wait_send()

    def all_copy(ref, send, recv, lead, k, slab, owner):
        index = (slice(None),) if lead else ()
        at = ref.at[index + (pl.ds(owner, 1),)]
        return remote(at, at, send.at[k], recv.at[k], slab)

    def all_start(*args):
        each(1, ns, lambda k: all_copy(*args, k, lax.rem(me + k, ns), me).start())

    def all_wait(*args):
        def wait(k):
            peer = lax.rem(me - k + ns, ns)
            all_copy(*args, k, peer, peer).wait_recv()

        each(1, ns, wait)

    def all_sent(*args):
        each(1, ns, lambda k: all_copy(*args, k, lax.rem(me + k, ns), me).wait_send())

    seed_part = seed_ref[0] * 277803737 + 1013904223
    hashed_place = place * 747796405
    first0 = me * cx - cx

    def logk_at(x_now):
        q = hashed_place + (x_now * (size0[0] * size0[1]) * 747796405 + seed_part)
        q = jnp.bitwise_xor(q, lax.shift_right_logical(q, jnp.full(size0, 15, jnp.int32)))
        q = q * 1274126177
        q = jnp.bitwise_xor(q, lax.shift_right_logical(q, jnp.full(size0, 13, jnp.int32)))
        low = jnp.bitwise_and(q, 65535)
        return 3.0 * (low.astype(F32) / 65536.0) - 1.5

    def logk_plane(p):
        x_now = first0 - 1 + p
        logk = logk_at(x_now)
        known = (x_now >= 0) & (x_now <= last0)
        e0[p] = jnp.where(known, jnp.exp(0.5 * logk), 0.0)
        ie0[p] = jnp.exp(-0.5 * logk)

    each(0, 3 * cx + 2, logk_plane)
    first1 = 2 * me - own1

    def logk1_plane(p):
        x_now = 2 * (first1 + p)
        l1[p] = restrict2(logk_at(x_now) + logk_at(x_now + 1), pad1) * 0.125

    each(own1, own1 + 2, logk1_plane)
    both_fields = right_mul(l1[own1] + l1[own1 + 1], pad2[1],
                            lambda i, j: half_of(i) == jnp.bitwise_and(j, size2[1] - 1), 3)
    l2[pl.ds(me, 1)] = (left_mul(both_fields, pad2[0], coarsen, 3) * 0.125)[None]
    all_start(l2, s_l2, r_l2, False)

    def operator0(p):
        x_now = first0 + p
        center = e0[p + 1]
        d = diag_plane(center, e0[p], e0[p + 2], x_now, last0, size0)
        known = (x_now >= 0) & (x_now <= last0)
        q = jnp.where(known, OMEGA / d, 0.0)
        d0[p] = d
        q0[p] = q
        g0[p] = q * center

    each(0, 3 * cx, operator0)

    def first0_c(p):
        q = q0[p]
        c0[0, p] = q * b0[0, p]
        c0[1, p] = q * b0[1, p]

    def first_sweeps(u, c, g, size, p):
        gain = g[p]

        def one(f):
            now = c[f, p]
            total = c[f, p - 1] + c[f, p + 1] + nsum(now, size)
            u[f, p] = (2.0 - OMEGA) * now + gain * total

        both(one)

    def sweep(u, c, g, out, size, p, gp=None, cp=None):
        gp = p if gp is None else gp
        cp = p if cp is None else cp
        gain = g[gp]

        def one(f):
            now = u[f, p]
            total = u[f, p - 1] + u[f, p + 1] + nsum(now, size)
            out[f, p] = (1.0 - OMEGA) * now + c[f, cp] + gain * total

        both(one)

    def residue(u, b, e, d, size, f, p, ep, dp, bp):
        now = u[f, p]
        total = u[f, p - 1] + u[f, p + 1] + nsum(now, size)
        return b[f, bp] + e[ep] * total - d[dp] * now

    each(cx, 2 * cx, first0_c)

    each(0, own1, logk1_plane)
    halo_pass(0)
    halo_pass(1)
    each(own1 + 2, 2 * own1 + 2, logk1_plane)
    each(cx + 1, 2 * cx - 1, functools.partial(first_sweeps, ua, c0, g0, size0))
    halo_wait(0)
    halo_wait(1)
    each(half, cx, first0_c)
    each(2 * cx, 2 * cx + half, first0_c)
    each(cx - 1, cx + 1, functools.partial(first_sweeps, ua, c0, g0, size0))
    each(2 * cx - 1, 2 * cx + 1, functools.partial(first_sweeps, ua, c0, g0, size0))

    for f in range(2):
        for i in range(2):
            p = cx + 2 * i
            pair = (residue(ua, b0, e0, d0, size0, f, p, p + 1, p, p)
                    + residue(ua, b0, e0, d0, size0, f, p + 1, p + 2, p + 1, p + 1))
            b1[f, own1 + i] = restrict2(pair, pad1) * 0.5
    near_start(b1, s_b1, r_b1, True)

    width1 = 2 * own1 + 2

    def exp1(p):
        x_now = first1 + p
        ok = inside(pad1, size1, x_now, last1)
        logk = l1[p]
        e1[p] = jnp.where(ok, jnp.exp(0.5 * logk), 0.0)
        ie1[p] = jnp.where(ok, jnp.exp(-0.5 * logk), 0.0)

    each(0, width1, exp1)

    def operator1(p):
        x_now = first1 + p
        center = e1[p]
        d = diag_plane(center, e1[p - 1], e1[p + 1], x_now, last1, size1)
        q = jnp.where(inside(pad1, size1, x_now, last1), OMEGA / d, 0.0)
        d1[p] = d
        q1[p] = q
        g1[p] = q * center

    each(1, width1 - 1, operator1)

    all_wait(l2, s_l2, r_l2, False)
    counts = [ns >> i for i in range(3)]
    for i in range(3):
        e, ie, d, q, g, c, u, w = coarse[i]
        size, pad, n = sizes[2 + i], pads[2 + i], counts[i]
        e[0] = jnp.zeros(pad, F32)
        e[n + 1] = jnp.zeros(pad, F32)
        for ref in (u, w):
            ref[0] = jnp.zeros(pad, F32)
            ref[n + 1] = jnp.zeros(pad, F32)

        def exps(p, e=e, ie=ie, size=size, pad=pad, n=n, i=i, d=d):
            if i == 0:
                logk = l2[p]
            else:
                above = coarse[i - 1][4] if i > 1 else l2
                logk = restrict2(above[2 * p] + above[2 * p + 1], pad, 3) * 0.125
                g_now = coarse[i][4]
                g_now[p] = logk
            ok = inside(pad, size, p, n - 1, 2)
            e[p + 1] = jnp.where(ok, jnp.exp(0.5 * logk), 0.0)
            ie[p] = jnp.where(ok, jnp.exp(-0.5 * logk), 0.0)

        each(0, n, exps)
    for i in range(3):
        e, ie, d, q, g, c, u, w = coarse[i]
        size, pad, n = sizes[2 + i], pads[2 + i], counts[i]

        def ops(p, e=e, d=d, q=q, g=g, size=size, pad=pad, n=n):
            center = e[p + 1]
            dd = diag_plane(center, e[p], e[p + 2], p, n - 1, size, 2)
            qq = jnp.where(inside(pad, size, p, n - 1, 2), OMEGA / dd, 0.0)
            d[p] = dd
            q[p] = qq
            g[p] = qq * center

        each(0, n, ops)

    def first1_c(p):
        q = q1[p]
        c1[0, p] = q * b1[0, p]
        c1[1, p] = q * b1[1, p]

    near_wait(b1, s_b1, r_b1, True, distances=(1,))
    each(own1 - 2, own1 + 4, first1_c)
    each(own1 - 1, own1 + 3, functools.partial(first_sweeps, va, c1, g1, size1))
    pairs = [(residue(va, b1, e1, d1, size1, f, own1, own1, own1, own1)
              + residue(va, b1, e1, d1, size1, f, own1 + 1, own1 + 1, own1 + 1, own1 + 1))
             for f in range(2)]
    side = [right_mul(pairs[f], pad2[1], lambda i, j, f=f: half_of(i) + f * size2[1] == j)
            for f in range(2)]
    b2[pl.ds(me, 1)] = (left_mul(side[0] + side[1], pad2[0], coarsen) * 0.5)[None]
    all_start(b2, s_b2, r_b2, False)
    halo_start(2)
    halo_start(3)

    near_wait(b1, s_b1, r_b1, True, distances=(2, 3))
    each(own1 - 5, own1 - 2, first1_c)
    each(own1 + 4, own1 + 7, first1_c)
    each(own1 - 4, own1 - 1, functools.partial(first_sweeps, va, c1, g1, size1))
    each(own1 + 3, own1 + 6, functools.partial(first_sweeps, va, c1, g1, size1))

    all_wait(b2, s_b2, r_b2, False)

    def solve(i, source):
        e, ie, d, q, g, c, u, w = coarse[i]
        size, pad, n = sizes[2 + i], pads[2 + i], counts[i]

        def begin(p):
            value = q[p] * source[p]
            c[p] = value
            u[p + 1] = value

        each(0, n, begin, 8)

        def full(src, dst):
            def one(p):
                now = src[p]
                total = src[p - 1] + src[p + 1] + nsum(now, size, 2)
                dst[p] = (1.0 - OMEGA) * now + c[p - 1] + g[p - 1] * total

            each(1, n + 1, one, 8)

        if i == 2:
            now, then = u, w
            for _ in range(COARSE_SWEEPS - 1):
                full(now, then)
                now, then = then, now
            return now
        full(u, w)
        below = (b3, b4)[i]

        def rest_of(p):
            now = w[p + 1]
            total = w[p] + w[p + 2] + nsum(now, size, 2)
            return source[p] + e[p + 1] * total - d[p] * now

        def down(p):
            below[p] = restrict2(rest_of(2 * p) + rest_of(2 * p + 1), pads[3 + i]) * 0.5

        each(0, counts[i + 1], down, 4)
        fix = solve(i + 1, below)
        fix_inv = coarse[i + 1][1]

        def up(p):
            add = prolong2(fix[p + 1] * fix_inv[p], pad)
            w[2 * p + 1] = w[2 * p + 1] + e[2 * p + 1] * add
            w[2 * p + 2] = w[2 * p + 2] + e[2 * p + 2] * add

        each(0, counts[i + 1], up, 4)
        full(w, u)
        full(u, w)
        return w

    top = solve(0, b2)
    top_inv = coarse[0][1]
    halo_pass(2)
    halo_pass(3)

    def correct1(k):
        at = jnp.clip(me - 2 + k, 0, ns - 1)
        p = own1 - 4 + 2 * k
        rows = left_mul(top[at + 1] * top_inv[at], pad1[0], refine)
        for f in range(2):
            add = right_mul(rows, pad1[1], lambda i, j, f=f: i == f * size2[1] + half_of(j))
            va[f, p] = va[f, p] + e1[p] * add
            va[f, p + 1] = va[f, p + 1] + e1[p + 1] * add

    each(0, 5, correct1)
    each(own1 - 3, own1 + 5, functools.partial(sweep, va, c1, g1, vb, size1))
    each(own1 - 2, own1 + 4, functools.partial(sweep, vb, c1, g1, va, size1))

    halo_wait(2)
    halo_wait(3)
    each(0, half, first0_c)
    each(2 * cx + half, 3 * cx, first0_c)
    each(1, cx - 1, functools.partial(first_sweeps, ua, c0, g0, size0))
    each(2 * cx + 1, 3 * cx - 1, functools.partial(first_sweeps, ua, c0, g0, size0))

    def correct0(f, l, planes):
        add = prolong2(va[f, l] * ie1[l], size0)
        for p in planes:
            ua[f, p] = ua[f, p] + e0[p + 1] * add

    for f in range(2):
        correct0(f, own1 - 2, (1,))
        correct0(f, own1 + 3, (3 * cx - 2,))

    def middle(k):
        p = 2 + 2 * k
        both(lambda f: correct0(f, own1 - 1 + k, (p, p + 1)))

    each(0, 4, middle)
    each(2, 3 * cx - 2, functools.partial(sweep, ua, c0, g0, ub, size0))
    each(3, 3 * cx - 3, functools.partial(sweep, ub, c0, g0, ua, size0))

    def heads(p):
        inv = ie0[p + 1]
        ub[0, p] = ua[0, p] * inv
        ub[1, p] = ua[1, p] * inv

    each(cx - 1, 2 * cx + 1, heads)

    iy, iz = iota(size0, 0), iota(size0, 1)
    y_end = (iy == 0) | (iy == size0[0] - 1)

    def gradient(p, carry):
        plain, by_y, by_z = carry
        h, a, e = ub[0, p], ub[1, p], e0[p + 1]
        head_ref[0, p - cx] = h
        adj_ref[0, p - cx] = a
        lower = e * e0[p] * (h - ub[0, p - 1]) * (a - ub[1, p - 1])
        upper = e * e0[p + 2] * (h - ub[0, p + 1]) * (a - ub[1, p + 1])
        x_now = first0 + p
        edge = 2.0 * ua[0, p] * ua[1, p]
        ends = jnp.where(x_now == 0, 1.0, 0.0) + jnp.where(x_now == last0, 1.0, 0.0)
        plain = plain + 0.5 * (lower + upper) + edge * (ends + jnp.where(y_end, 1.0, 0.0))
        by_y = by_y + e * roll(e, 1, 0) * (h - roll(h, 1, 0)) * (a - roll(a, 1, 0))
        by_z = by_z + e * roll(e, 1, 1) * (h - roll(h, 1, 1)) * (a - roll(a, 1, 1))
        return plain, by_y, by_z

    plain, by_y, by_z = lax.fori_loop(cx, 2 * cx, gradient, (zero0, zero0, zero0))
    by_y = jnp.where(iy > 0, by_y, 0.0)
    by_z = jnp.where(iz > 0, by_z, 0.0)
    cells = plain + 0.5 * (by_y + roll(by_y, -1, 0) + by_z + roll(by_z, -1, 1))
    zy, zz = zone_ref.shape[1:]
    quarter = lambda i, j: jnp.right_shift(i, 2) == j
    zone = right_mul(left_mul(cells, zy, quarter, 3), zz, quarter, 3)
    weight_sum = weight_ref[0]
    for w in range(1, weight_ref.shape[0]):
        weight_sum = weight_sum + weight_ref[w]
    own = jnp.full(zone.shape, weight_ref[node], jnp.int32).astype(F32)
    portion = own / jnp.full(zone.shape, weight_sum, jnp.int32).astype(F32)
    own_zone[...] = -(portion * zone)
    zone_copy = pltpu.make_async_remote_copy(
        src_ref=own_zone, dst_ref=other_zone, send_sem=s_z, recv_sem=r_z,
        device_id={"node": 1 - node}, device_id_type=pl.DeviceIdType.MESH)
    zone_copy.start()

    for i in range(4):
        halo_sent(i)

    near_sent(b1, s_b1, r_b1, True)
    all_sent(l2, s_l2, r_l2, False)
    all_sent(b2, s_b2, r_b2, False)
    zone_copy.wait()
    zone_ref[0] = own_zone[...] + other_zone[...]
    KEPT.clear()


def body(ns, field_seeds, quad_weight, recharge, well_cells, well_rates, sensitivity):
    cx, ny, nz = recharge.shape
    sizes = [(ny >> l, nz >> l) for l in range(LEVELS)]
    pads = [(max(y, 8), max(z, 128)) for y, z in sizes]
    wide = 3 * cx
    near = 4 * REACH + 2
    vmem, smem = pltpu.VMEM, pltpu.SMEM
    p0, p1, p2 = pads[:3]
    dma = pltpu.SemaphoreType.DMA
    scratch = [
        vmem((2, wide) + p0, F32), vmem((wide + 2,) + p0, F32), vmem((wide,) + p0, F32),
        vmem((wide,) + p0, F32), vmem((wide,) + p0, F32), vmem((2, wide) + p0, F32),
        vmem((2, wide) + p0, F32), vmem((2, wide) + p0, F32),
        vmem((wide + 2,) + p0, F32), vmem((ns // 2,) + pads[3], F32),
        vmem((2, near) + p1, F32), vmem((near,) + p1, F32), vmem((near,) + p1, F32),
        vmem((near,) + p1, F32), vmem((near,) + p1, F32), vmem((near,) + p1, F32),
        vmem((near,) + p1, F32), vmem((2, near) + p1, F32), vmem((2, near) + p1, F32),
        vmem((2, near) + p1, F32), vmem((ns // 4,) + pads[4], F32),
        vmem((ns,) + p2, F32), vmem((ns,) + p2, F32),
    ]
    for i in range(3):
        n, pad = ns >> i, pads[2 + i]
        scratch += [vmem((n + 2,) + pad, F32), vmem((n,) + pad, F32), vmem((n,) + pad, F32),
                    vmem((n,) + pad, F32), vmem((n,) + pad, F32), vmem((n,) + pad, F32),
                    vmem((n + 2,) + pad, F32), vmem((n + 2,) + pad, F32)]
    zone = (ny // 4, nz // 4)
    scratch += [vmem(zone, F32), vmem(zone, F32)]
    spread = 2 * REACH + 1
    scratch += [dma((8,)), dma((8,)), dma((2,)), dma((spread,)), dma((spread,)),
                dma((ns,)), dma((ns,)), dma((ns,)), dma((ns,)), dma, dma]
    in_v, in_s = pl.BlockSpec(memory_space=vmem), pl.BlockSpec(memory_space=smem)
    field = jax.ShapeDtypeStruct((1, cx, ny, nz), F32)
    return pl.pallas_call(
        functools.partial(kernel, ns, sizes, pads),
        out_shape=(field, field, jax.ShapeDtypeStruct((1,) + zone, F32)),
        in_specs=[in_s, in_s, pl.BlockSpec(memory_space=pl.ANY), in_s, in_s,
                  pl.BlockSpec(memory_space=pl.ANY)],
        out_specs=(in_v, in_v, in_v),
        scratch_shapes=scratch,
        compiler_params=pltpu.CompilerParams(
            collective_id=0, has_side_effects=True, vmem_limit_bytes=48 * 1024 * 1024),
    )(field_seeds, quad_weight, recharge, well_cells, well_rates, sensitivity)


def solution(mesh):
    placed = (
        P(("groups", "node")),
        P("groups"),
        P(("groups", "slab"), None, None),
        P(("groups", "slab")),
        P(("groups", "slab")),
        P(("groups", "slab"), None, None),
    )
    return jax.shard_map(
        functools.partial(body, mesh.shape["slab"]),
        mesh=mesh,
        in_specs=placed,
        out_specs=(
            P(("groups", "node"), "slab", None, None),
            P(("groups", "node"), "slab", None, None),
            P(("groups", "slab"), None, None),
        ),
        check_vma=False,
    )
```
